128 devices in a mesh: cell: 32 (over x, y, core), gene: 4 (over z).
Axes of the slice: x: 4, y: 4, z: 4, core: 2. Of those that a mesh axis runs over, the one named last changes fastest.
Arguments:
- counts: float32 [65536, 8192], P('cell', 'gene'), may hold values from 0 to 9, as said below
- donors: int32 [65536], P('cell'), may hold values from 0 to 127
- offset_table: int32 [128], replicated, may hold values from -8 to 8
- factors: float32 [64, 65536], P(None, 'cell'), may hold values from -2.4 to 2.4
- factor_mean: float32 [64, 65536], P(None, 'cell'), may hold values from -1.2 to 1.2
- factor_var: float32 [64, 65536], P(None, 'cell'), may hold values from 0.006 to 4, as said below
- loadings: float32 [64, 8192], P(None, 'gene'), may hold values from -1.5 to 1.5
- loading_mean: float32 [64, 8192], P(None, 'gene'), may hold values from -1.2 to 1.2
- loading_var: float32 [64, 8192], P(None, 'gene'), may hold values from 0.006 to 4, as said below
Outputs:
- new_factors: float32 [64, 65536], P(None, 'cell')
- new_factor_mean: float32 [64, 65536], P(None, 'cell')
- new_factor_var: float32 [64, 65536], P(None, 'cell')
- new_loadings: float32 [64, 8192], P(None, 'gene')
- new_loading_mean: float32 [64, 8192], P(None, 'gene')
- new_loading_var: float32 [64, 8192], P(None, 'gene')
The draws below stay inside these ranges and needn't reach their ends.
Inputs may be any that keep to these rules, and one draw needn't show every extreme that they name: `counts`: whole numbers, products of two whole numbers from 0 to 3. `factor_var`: positive. `loading_var`: positive.
All inputs are finite; a program needn't handle non-finite values.
Results may differ from the reference program's by a relative error of at most 0.0003.
Values sent between devices are 32-bit elements; how exact they have to be, the bound alone decides.
No kernel may reach another device: no remote copies, remote signals or barrier semaphores. Data moves between devices by JAX's collectives and lax.ppermute only.
A program may use at most 128 MiB of HBM per device.

```python
import math
import jax
import jax.numpy as jnp
from jax import lax

FACTORS = 64
GENES = 8192
DONORS = 128
CELL_DEV = 2048
ROUNDS = 2
CELLS = 65536


def draw_counts(key, part):
    key = jax.random.fold_in(key, 1)
    levels = jax.random.randint(key, (CELLS, GENES), 0, 16)
    return (levels // 4 * (levels % 4)).astype(jnp.float32)


def draw_factor_var(key, part):
    key = jax.random.fold_in(key, 2)
    first, second, third = jax.random.split(key, 3)
    entry = jnp.exp(math.log(2.0) * jax.random.uniform(first, (FACTORS, CELLS), jnp.float32))
    across = jnp.exp(math.log(10.0) * jax.random.uniform(second, (FACTORS, 1), jnp.float32))
    along = jnp.exp(math.log(10.0) * jax.random.uniform(third, (1, CELLS), jnp.float32))
    place = jnp.arange(CELLS, dtype=jnp.float32)[None, :] / float(CELLS)
    return 0.02 * entry * across * along * jnp.exp(-math.log(3.0) * place)


def draw_loading_var(key, part):
    key = jax.random.fold_in(key, 3)
    first, second, third = jax.random.split(key, 3)
    entry = jnp.exp(math.log(2.0) * jax.random.uniform(first, (FACTORS, GENES), jnp.float32))
    across = jnp.exp(math.log(10.0) * jax.random.uniform(second, (FACTORS, 1), jnp.float32))
    along = jnp.exp(math.log(10.0) * jax.random.uniform(third, (1, GENES), jnp.float32))
    place = jnp.arange(GENES, dtype=jnp.float32)[None, :] / float(GENES)
    return 0.02 * entry * across * along * jnp.exp(-math.log(3.0) * place)


def spread_entries(key, rows, columns, deviation):
    return deviation * jax.random.truncated_normal(key, -6.0, 6.0, (rows, columns), jnp.float32)


def draw_factors(key, part):
    key = jax.random.fold_in(key, 4)
    return spread_entries(key, FACTORS, CELLS, 0.4)


def draw_loadings(key, part):
    key = jax.random.fold_in(key, 5)
    return spread_entries(key, FACTORS, GENES, 0.25)


def place_ends(values, stream_key, least, top_value):
    longest = values.shape.index(max(values.shape))
    spots = []
    for shift in (0, 1):
        where = [jax.random.randint(jax.random.fold_in(stream_key, axis), (), 0, length) for axis, length in enumerate(values.shape)]
        where[longest] = (where[longest] + shift) % values.shape[longest]
        spots.append(tuple(where))
    return values.at[spots[0]].set(least).at[spots[1]].set(top_value)


def level_of(stream_key, extent, pieces, least, high):
    def one(axis_at, blocks):
        heights = jax.random.uniform(jax.random.fold_in(jax.random.fold_in(stream_key, 6), axis_at), (blocks,), jnp.float32, least / len(pieces), high / len(pieces))
        return jnp.repeat(jnp.exp(heights), extent[axis_at] // blocks).reshape((-1,) + (1,) * (len(extent) - axis_at - 1))

    gain = one(*pieces[0])
    for cut in pieces[1:]:
        gain = gain * one(*cut)
    return gain


def noise(key, shape, spread, bound, shards=(), held_as=jnp.bfloat16):
    array = jax.random.normal(key, shape, jnp.float32) * spread
    if len(shards) > 0:
        array = level_of(key, shape, shards, -0.22, 0.18) * array
    return jnp.clip(array, min=-bound, max=bound).astype(held_as)


def setup_inputs(seed: int = 0) -> dict:
    seeds = jax.random.split(jax.random.key(seed), 10)
    counts = draw_counts(jax.random.fold_in(seeds[9], 71), 0)
    donors = place_ends(jax.random.randint(seeds[1], (CELLS,), 0, DONORS), jax.random.fold_in(seeds[1], 1), 0, DONORS - 1).astype(jnp.int32)
    offset_table = place_ends(jax.random.randint(seeds[2], (DONORS,), -8, 9), jax.random.fold_in(seeds[2], 1), -8, 8).astype(jnp.int32)
    factors = draw_factors(jax.random.fold_in(seeds[9], 71), 0)
    factor_mean = noise(seeds[4], (FACTORS, CELLS), 0.2, 1.2, ((1, 32),), jnp.float32)
    factor_var = draw_factor_var(jax.random.fold_in(seeds[9], 71), 0)
    loadings = draw_loadings(jax.random.fold_in(seeds[9], 71), 0)
    loading_mean = noise(seeds[7], (FACTORS, GENES), 0.2, 1.2, ((1, 4),), jnp.float32)
    loading_var = draw_loading_var(jax.random.fold_in(seeds[9], 71), 0)
    return {"counts": counts, "donors": donors, "offset_table": offset_table, "factors": factors, "factor_mean": factor_mean, "factor_var": factor_var, "loadings": loadings, "loading_mean": loading_mean, "loading_var": loading_var}


decay_first = 0.9
decay_second = 0.999
epsilon = 1e-06
rate_factors = 0.2
rate_loadings = 0.2
offset_unit = 0.125

def inverse_root(variance):
    return 1.0 / (jnp.sqrt(variance) + epsilon)

def moment_step(values, mean_old, var_old, gradient, scale, total, entries, rate):
    mean_new = decay_first * mean_old + (1.0 - decay_first) * gradient
    factor = rate / jnp.sqrt(total / entries)
    values_new = values - factor * mean_new * scale
    var_new = decay_second * var_old + (1.0 - decay_second) * gradient * gradient
    return (values_new, mean_new, var_new)

def reference(counts, donors, offset_table, factors, factor_mean, factor_var, loadings, loading_mean, loading_var):
    offsets = offset_unit * offset_table[donors].astype(jnp.float32)
    blocks = CELLS // CELL_DEV
    indices = jnp.arange(blocks, dtype=jnp.int32)
    highest = lax.Precision.HIGHEST

    def residual_block(current, load, index):
        begin = (index * CELL_DEV).astype(jnp.int32)
        part = lax.dynamic_slice_in_dim(current, begin, CELL_DEV, 1)
        rows = lax.dynamic_slice_in_dim(counts, begin, CELL_DEV, 0)
        shifts = lax.dynamic_slice_in_dim(offsets, begin, CELL_DEV, 0)
        linear = lax.dot_general(part, load, (((0,), (0,)), ((), ())), precision=highest) + shifts[:, None]
        return (part, jnp.exp(linear) - rows)
    for repeat in range(ROUNDS):

        def factor_block(index):
            part, tile = residual_block(factors, loadings, index)
            return lax.dot_general(loadings, tile, (((1,), (1,)), ((), ())), precision=highest) / jnp.sqrt(float(GENES))
        stacked = lax.map(factor_block, indices)
        grad_factors = jnp.transpose(stacked, (1, 0, 2)).reshape(FACTORS, CELLS)
        fac_scale = inverse_root(factor_var)
        factors, factor_mean, factor_var = moment_step(factors, factor_mean, factor_var, grad_factors, fac_scale, jnp.sum(fac_scale * fac_scale), float(CELLS * FACTORS), rate_factors)

        def loading_block(total, index):
            part, tile = residual_block(factors, loadings, index)
            return (total + lax.dot_general(part, tile, (((1,), (0,)), ((), ())), precision=highest) / jnp.sqrt(float(CELLS)), None)
        grad_loadings, unused = lax.scan(loading_block, jnp.zeros((FACTORS, GENES), jnp.float32), indices)
        load_scale = inverse_root(loading_var)
        loadings, loading_mean, loading_var = moment_step(loadings, loading_mean, loading_var, grad_loadings, load_scale, jnp.sum(load_scale * load_scale), float(GENES * FACTORS), rate_loadings)
    return (factors, factor_mean, factor_var, loadings, loading_mean, loading_var)
```

```python
import functools
import math

import jax
import jax.numpy as jnp
from jax import lax
from jax.experimental import pallas as pl
from jax.experimental.pallas import tpu as pltpu
from jax.sharding import PartitionSpec as P

decay_first = 0.9
decay_second = 0.999
epsilon = 1e-06
rate_factors = 0.2
rate_loadings = 0.2
offset_unit = 0.125
LOG2E = math.log2(math.e)
LANES = 128
SUB = 8
DEPTH = 256
f32 = jnp.float32
bf16 = jnp.bfloat16
VMEM_LIMIT = 20 << 20
CELL_BLOCK = 512
GENE_BLOCK = 256
CHUNK = 256


def split(x):
    high = x.astype(bf16)
    return high, (x - high.astype(f32)).astype(bf16)


def inverse_root(variance):
    return 1.0 / (jnp.sqrt(variance) + epsilon)


def square_tile(scale):
    square = scale * scale
    total = None
    for r in range(0, scale.shape[0], SUB):
        for c in range(0, scale.shape[1], LANES):
            part = square[r : r + SUB, c : c + LANES]
            total = part if total is None else total + part
    return total


def cell_operand(f, off):
    high, low = split(f)
    first = off.astype(bf16).astype(f32)
    rest = off - first
    second = rest.astype(bf16).astype(f32)
    third = rest - second
    row = lax.broadcasted_iota(jnp.int32, f.shape, 0)
    extra = jnp.where(row == 0, first, jnp.where(row == 1, second, jnp.where(row == 2, third, 0.0)))
    return high, low, jnp.concatenate([high, high, low, extra.astype(bf16)], 0)


def gene_operand(l):
    high, low = split(l * LOG2E)
    row = lax.broadcasted_iota(jnp.int32, l.shape, 0)
    ones = jnp.where(row < 3, 1.0, 0.0).astype(bf16)
    return jnp.concatenate([high, low, high, ones], 0)


def offsets_of(donors, table):
    which = lax.broadcasted_iota(jnp.int32, (table.shape[0], donors.shape[1]), 0)
    picked = jnp.where(which == donors, table.astype(f32), 0.0)
    return jnp.sum(picked, axis=0, keepdims=True) * (offset_unit * LOG2E)


def set_loads(l, load_cat, load_hl):
    load_cat[...] = gene_operand(l)
    high, low = split(l)
    load_hl[...] = jnp.concatenate([high, low], 0).T


def cell_pass(f_ref, off_ref, load_cat, load_hl, counts, g_ref, genes_total, ready=None):
    width, cells = f_ref.shape

    def block(b, _):
        if ready is not None:
            ready(b)
        at = pl.ds(pl.multiple_of(b * CELL_BLOCK, CELL_BLOCK), CELL_BLOCK)
        _, _, cat = cell_operand(f_ref[:, at], off_ref[:, at])
        lhs = cat.T
        total = None
        for g in range(0, load_cat.shape[1], CHUNK):
            of = slice(g, g + CHUNK)
            lin = jnp.dot(lhs, load_cat[:, of], preferred_element_type=f32)
            high, low = split(jnp.exp2(lin) - counts[at, of])
            part = jnp.dot(high, load_hl[of, :], preferred_element_type=f32)
            part += jnp.dot(low, load_hl[of, :], preferred_element_type=f32)
            total = part if total is None else total + part
        total = total.T
        grad = (total[:width] + total[width:]) * (1.0 / math.sqrt(genes_total))
        rows = CELL_BLOCK // LANES * width
        grad = jnp.concatenate([grad[:, c : c + LANES] for c in range(0, CELL_BLOCK, LANES)], 0)
        g_ref[pl.ds(pl.multiple_of(b * rows, rows), rows), :] = grad
        return 0

    lax.fori_loop(0, cells // CELL_BLOCK, block, 0)


def gene_pass(l_ref, cell_cat, cell_hl, counts, g_ref, cells_total):
    width, genes = l_ref.shape
    cells = cell_cat.shape[0]
    half = genes // GENE_BLOCK // 2
    rows = GENE_BLOCK // LANES * width

    def block(b, _):
        at = pl.ds(pl.multiple_of(b * GENE_BLOCK, GENE_BLOCK), GENE_BLOCK)
        load = gene_operand(l_ref[:, at])
        total = None
        for c in range(0, cells, CHUNK):
            of = slice(c, c + CHUNK)
            lin = jnp.dot(cell_cat[of, :], load, preferred_element_type=f32)
            resid = (jnp.exp2(lin) - counts[of, at]).astype(bf16)
            part = jnp.dot(cell_hl[:, of], resid, preferred_element_type=f32)
            total = part if total is None else total + part
        grad = (total[:width] + total[width:]) * (1.0 / math.sqrt(cells_total))
        grad = jnp.concatenate([grad[:, c : c + LANES] for c in range(0, GENE_BLOCK, LANES)], 0)
        g_ref[b // half, pl.ds(pl.multiple_of(b % half * rows, rows), rows), :] = grad
        return 0

    lax.fori_loop(0, 2 * half, block, 0)


def move(refs, grad_row, total, entries, rate, outs):
    values_ref, mean_ref, var_ref = refs
    width, length = values_ref.shape
    factor = rate / jnp.sqrt(total / entries)
    tile = None
    for c in range(0, length, LANES):
        at = slice(c, c + LANES)
        gradient = grad_row(c // LANES)
        var_old = var_ref[:, at]
        mean = decay_first * mean_ref[:, at] + (1.0 - decay_first) * gradient
        var = decay_second * var_old + (1.0 - decay_second) * gradient * gradient
        outs[0][:, at] = values_ref[:, at] - factor * mean * inverse_root(var_old)
        outs[1][:, at] = mean
        outs[2][:, at] = var
        part = square_tile(inverse_root(var))
        tile = part if tile is None else tile + part
    return tile


def total_kernel(var_ref, tile_ref):
    tile_ref[...] = square_tile(inverse_root(var_ref[...]))


def first_kernel(
    donors_ref, table_ref, f_ref, l_ref, lv_ref, counts_hbm, g_ref, off_ref, counts_ref, load_cat, load_hl, sems, *, genes_total
):
    cells = f_ref.shape[1]
    copies = []
    for b in range(cells // CELL_BLOCK):
        at = pl.ds(b * CELL_BLOCK, CELL_BLOCK)
        copies.append(pltpu.make_async_copy(counts_hbm.at[at], counts_ref.at[at], sems.at[b]))
        copies[-1].start()
    off_ref[...] = offsets_of(donors_ref[...], table_ref[...])
    set_loads(l_ref[...], load_cat, load_hl)
    rows = f_ref.shape[0] * cells // LANES
    g_ref[rows : rows + SUB, :] = square_tile(inverse_root(lv_ref[...]))

    def ready(b):
        at = pl.ds(pl.multiple_of(b * CELL_BLOCK, CELL_BLOCK), CELL_BLOCK)
        pltpu.make_async_copy(counts_hbm.at[at], counts_ref.at[at], sems.at[b]).wait()

    cell_pass(f_ref, off_ref, load_cat, load_hl, counts_ref, g_ref, genes_total, ready)


def gene_kernel(
    tile_ref, f_ref, fm_ref, fv_ref, grad_ref, off_ref, l_ref, counts_ref,
    g_ref, nf_ref, nm_ref, nv_ref, cell_cat, cell_hl, *, cells_total
):
    width, cells = f_ref.shape
    tile = move(
        (f_ref, fm_ref, fv_ref), lambda c: grad_ref[c * width : (c + 1) * width, :], jnp.sum(tile_ref[...]),
        cells_total * width, rate_factors, (nf_ref, nm_ref, nv_ref),
    )
    rows = g_ref.shape[1]
    for h in range(2):
        g_ref[h, rows - SUB : rows, :] = tile
    high, low, cat = cell_operand(nf_ref[...], off_ref[...])
    cell_cat[...] = cat.T
    cell_hl[...] = jnp.concatenate([high, low], 0)
    gene_pass(l_ref, cell_cat, cell_hl, counts_ref, g_ref, cells_total)


def grad_of_halves(grad_ref, width):
    per = (grad_ref.shape[1] - SUB) // width
    return lambda c: grad_ref[c // per, c % per * width : (c % per + 1) * width, :]


def cell_kernel(
    tile_ref, l_ref, lm_ref, lv_ref, grad_ref, f_ref, off_ref, counts_ref,
    g_ref, nl_ref, nm_ref, nv_ref, load_cat, load_hl, *, genes_total
):
    width, genes = l_ref.shape
    tile = move(
        (l_ref, lm_ref, lv_ref), grad_of_halves(grad_ref, width), jnp.sum(tile_ref[...]),
        genes_total * width, rate_loadings, (nl_ref, nm_ref, nv_ref),
    )
    rows = g_ref.shape[0]
    g_ref[rows - SUB : rows, :] = tile
    set_loads(nl_ref[...], load_cat, load_hl)
    cell_pass(f_ref, off_ref, load_cat, load_hl, counts_ref, g_ref, genes_total)


def last_kernel(tile_ref, l_ref, lm_ref, lv_ref, grad_ref, nl_ref, nm_ref, nv_ref, *, genes_total):
    width, genes = l_ref.shape
    move(
        (l_ref, lm_ref, lv_ref), grad_of_halves(grad_ref, width), jnp.sum(tile_ref[...]),
        genes_total * width, rate_loadings, (nl_ref, nm_ref, nv_ref),
    )


def exchange(value, partner):
    pairs = []
    for cell in range(32):
        for z in range(4):
            x, y, core, depth = partner(cell // 8, cell // 2 % 4, cell % 2, z)
            pairs.append((cell * 4 + z, ((x * 4 + y) * 2 + core) * 4 + depth))
    return lax.ppermute(value, ("cell", "gene"), pairs)


def near(i):
    return i ^ 1


def far(i):
    return 3 - i


def other_core(value):
    return exchange(value, lambda x, y, core, z: (x, y, 1 - core, z))


def along_cells(step):
    turn = near if step % 2 == 0 else far

    def partner(x, y, core, z):
        if (step // 2 + core) % 2 == 0:
            return turn(x), y, core, z
        return x, turn(y), core, z

    return partner


def along_genes(step):
    def partner(x, y, core, z):
        return x, y, core, (near if (step + core) % 2 == 0 else far)(z)

    return partner


def sum_over_genes(value):
    for step in range(2):
        value = value + exchange(value, along_genes(step))
    return value


def sum_over_chips(value):
    for step in range(4):
        value = value + exchange(value, along_cells(step))
    return value


def sum_over_cells(halves):
    core = lax.axis_index("cell") % 2
    mine = lax.dynamic_index_in_dim(halves, core, 0, keepdims=False)
    theirs = lax.dynamic_index_in_dim(halves, 1 - core, 0, keepdims=False)
    mine = sum_over_chips(mine + other_core(theirs))
    theirs = other_core(mine)
    return jnp.stack([jnp.where(core == 0, mine, theirs), jnp.where(core == 0, theirs, mine)])


def on_device(counts, donors, offset_table, factors, factor_mean, factor_var, loadings, loading_mean, loading_var):
    width, cells = factors.shape
    genes = loadings.shape[1]
    cells_total = float(cells * lax.axis_size("cell"))
    genes_total = float(genes * lax.axis_size("gene"))
    vmem = pl.BlockSpec(memory_space=pltpu.VMEM)
    like = lambda *shape: jax.ShapeDtypeStruct(shape, f32)
    cell_rows = width * cells // LANES + SUB
    gene_rows = width * genes // LANES // 2 + SUB
    cell_scratch = [pltpu.VMEM((DEPTH, genes), bf16), pltpu.VMEM((genes, 2 * width), bf16)]
    gene_scratch = [pltpu.VMEM((cells, DEPTH), bf16), pltpu.VMEM((2 * width, cells), bf16)]
    flops = 2 * (2 * DEPTH) * cells * genes

    def call(kernel, name, ins, outs, scratch=(), in_specs=None, work=1):
        return pl.pallas_call(
            kernel,
            name=name,
            in_specs=in_specs or [vmem] * len(ins),
            out_specs=[vmem] * len(outs),
            out_shape=outs,
            scratch_shapes=list(scratch),
            compiler_params=pltpu.CompilerParams(vmem_limit_bytes=VMEM_LIMIT),
            cost_estimate=pl.CostEstimate(
                flops=flops * work, bytes_accessed=4 * width * cells, transcendentals=cells * genes * work
            ),
        )(*ins)

    (fac_tile,) = call(total_kernel, "factor_scale_total", [factor_var], [like(SUB, LANES)], work=0)
    fac_tile = fac_tile + other_core(fac_tile)
    fac_tile = sum_over_chips(fac_tile)
    grad, off, held = call(
        functools.partial(first_kernel, genes_total=genes_total),
        "cell_pass_first",
        [donors.reshape(1, cells), offset_table.reshape(-1, 1), factors, loadings, loading_var, counts],
        [like(cell_rows, LANES), like(1, cells), pltpu.VMEM((cells, genes), f32)],
        cell_scratch + [pltpu.SemaphoreType.DMA((cells // CELL_BLOCK,))],
        [vmem] * 5 + [pl.BlockSpec(memory_space=pl.ANY)],
    )
    grad = sum_over_genes(grad)
    load_tile = grad[-SUB:]

    def loading_gradient(fac_tile, f, fm, fv, grad, l):
        return call(
            functools.partial(gene_kernel, cells_total=cells_total),
            "gene_pass",
            [fac_tile, f, fm, fv, grad, off, l, held],
            [like(2, gene_rows, LANES)] + [like(width, cells)] * 3,
            gene_scratch,
        )

    grad_l, f, fm, fv = loading_gradient(fac_tile, factors, factor_mean, factor_var, grad, loadings)
    grad_l = sum_over_cells(grad_l)
    fac_tile = grad_l[0, -SUB:]
    grad, l, lm, lv = call(
        functools.partial(cell_kernel, genes_total=genes_total),
        "cell_pass",
        [load_tile, loadings, loading_mean, loading_var, grad_l, f, off, held],
        [like(cell_rows, LANES)] + [like(width, genes)] * 3,
        cell_scratch,
    )
    grad = sum_over_genes(grad)
    load_tile = grad[-SUB:]
    grad_l, f, fm, fv = loading_gradient(fac_tile, f, fm, fv, grad, l)
    grad_l = sum_over_cells(grad_l)
    l, lm, lv = call(
        functools.partial(last_kernel, genes_total=genes_total),
        "loading_move",
        [load_tile, l, lm, lv, grad_l],
        [like(width, genes)] * 3,
        work=0,
    )
    return f, fm, fv, l, lm, lv


def solution(mesh):
    by_cell, by_gene = P(None, "cell"), P(None, "gene")
    return jax.shard_map(
        on_device,
        mesh=mesh,
        in_specs=(P("cell", "gene"), P("cell"), P(), by_cell, by_cell, by_cell, by_gene, by_gene, by_gene),
        out_specs=(by_cell, by_cell, by_cell, by_gene, by_gene, by_gene),
        check_vma=False,
    )
```

```python
import functools
import math

import jax
import jax.numpy as jnp
from jax import lax
from jax.experimental import pallas as pl
from jax.experimental.pallas import tpu as pltpu
from jax.sharding import PartitionSpec as P

decay_first = 0.9
decay_second = 0.999
epsilon = 1e-06
rate_factors = 0.2
rate_loadings = 0.2
offset_unit = 0.125
LOG2E = math.log2(math.e)
LANES = 128
SUB = 8
DEPTH = 256
f32 = jnp.float32
bf16 = jnp.bfloat16
LOW = False
CELL_BLOCK = 512
GENE_BLOCK = 256
COPY_CELLS = 256
PARTS = 2
CHUNK = 512


def split(x):
    high = x.astype(bf16)
    return high, (x - high.astype(f32)).astype(bf16)


def inverse_root(variance):
    return 1.0 / (jnp.sqrt(variance) + epsilon)


def square_tile(scale):
    square = scale * scale
    total = None
    for r in range(0, scale.shape[0], SUB):
        for c in range(0, scale.shape[1], LANES):
            part = square[r : r + SUB, c : c + LANES]
            total = part if total is None else total + part
    return total


def cell_operand(f, off):
    high, low = split(f)
    first = off.astype(bf16).astype(f32)
    rest = off - first
    second = rest.astype(bf16).astype(f32)
    third = rest - second
    row = lax.broadcasted_iota(jnp.int32, f.shape, 0)
    extra = jnp.where(row == 0, first, jnp.where(row == 1, second, jnp.where(row == 2, third, 0.0)))
    return high, low, jnp.concatenate([high, high, low, extra.astype(bf16)], 0)


def gene_operand(l):
    high, low = split(l * LOG2E)
    row = lax.broadcasted_iota(jnp.int32, l.shape, 0)
    ones = jnp.where(row < 3, 1.0, 0.0).astype(bf16)
    return jnp.concatenate([high, low, high, ones], 0)


def offsets_of(donors, table):
    column = jnp.broadcast_to(table.astype(f32), (LANES, table.shape[1])).T[:, :1]
    which = lax.broadcasted_iota(jnp.int32, (table.shape[1], donors.shape[1]), 0)
    picked = jnp.where(which == donors, column, 0.0)
    return jnp.sum(picked, axis=0, keepdims=True) * (offset_unit * LOG2E)


def set_loads(l, load_cat, load_hl):
    load_cat[...] = gene_operand(l)
    high, low = split(l)
    load_hl[...] = jnp.concatenate([high, low], 0)


def set_cells(f, off, cell_cat, cell_hl):
    high, low, cat = cell_operand(f, off)
    cell_cat[...] = cat.T
    cell_hl[...] = jnp.concatenate([high, low], 0)


def lane_rows(grad):
    return jnp.concatenate([grad[:, c : c + LANES] for c in range(0, grad.shape[1], LANES)], 0)


def wait_all(copies):
    for copy in copies:
        copy.wait()


def start_all(copies):
    for copy in copies:
        copy.start()
    return copies


def cell_pass(f_ref, off_ref, load_cat, load_hl, counts, stream, g_refs, genes_total):
    width, cells = f_ref.shape
    blocks = cells // CELL_BLOCK
    rows = width * CELL_BLOCK // LANES
    last = (((1,), (1,)), ((), ()))
    for b in range(blocks):
        at = slice(b * CELL_BLOCK, (b + 1) * CELL_BLOCK)
        _, _, cat = cell_operand(f_ref[:, at], off_ref[:, at])
        lhs = cat.T
        if stream is not None:
            stream(b)
        total, small = None, None
        for g in range(0, load_cat.shape[1], CHUNK):
            of = slice(g, g + CHUNK)
            lin = jnp.dot(lhs, load_cat[:, of], preferred_element_type=f32)
            high, low = split(jnp.exp2(lin) - counts[at, of].astype(f32))
            part = lax.dot_general(load_hl[:, of], high, last, preferred_element_type=f32)
            total = part if total is None else total + part
            if LOW:
                part = lax.dot_general(load_hl[:width, of], low, last, preferred_element_type=f32)
                small = part if small is None else small + part
        grad = total[:width] + total[width:]
        if LOW:
            grad += small
        half = blocks // 2
        g_refs[b // half][b % half * rows : (b % half + 1) * rows, :] = lane_rows(grad * (1.0 / math.sqrt(genes_total)))


def gene_pass(l_ref, cell_cat, cell_hl, counts, g_refs, cells_total):
    width, genes = l_ref.shape
    blocks = genes // GENE_BLOCK
    rows = width * GENE_BLOCK // LANES
    quarter = blocks // 4
    for b in range(blocks):
        at = slice(b * GENE_BLOCK, (b + 1) * GENE_BLOCK)
        load = gene_operand(l_ref[:, at])
        total = None
        for c in range(0, cell_cat.shape[0], CHUNK):
            of = slice(c, c + CHUNK)
            lin = jnp.dot(cell_cat[of, :], load, preferred_element_type=f32)
            resid = (jnp.exp2(lin) - counts[of, at].astype(f32)).astype(bf16)
            part = jnp.dot(cell_hl[:, of], resid, preferred_element_type=f32)
            total = part if total is None else total + part
        grad = (total[:width] + total[width:]) * (1.0 / math.sqrt(cells_total))
        q = b // quarter
        g_refs[q // 2][q % 2, b % quarter * rows : (b % quarter + 1) * rows, :] = lane_rows(grad)


def move(held, grad_row, total, entries, rate, moved):
    factor = rate / jnp.sqrt(total / entries)
    tile = None
    for c in range(0, moved.shape[2], LANES):
        at = slice(c, c + LANES)
        gradient = grad_row(c // LANES)
        var_old = held[2][:, at]
        mean = decay_first * held[1][:, at] + (1.0 - decay_first) * gradient
        var = decay_second * var_old + (1.0 - decay_second) * gradient * gradient
        moved[0, :, at] = held[0][:, at] - factor * mean * inverse_root(var_old)
        moved[1, :, at] = mean
        moved[2, :, at] = var
        part = square_tile(inverse_root(var))
        tile = part if tile is None else tile + part
    return tile


def total_kernel(var_hbm, tile_ref, var_ref, sem):
    copy = pltpu.make_async_copy(var_hbm, var_ref, sem)
    copy.start()
    copy.wait()
    tile_ref[...] = square_tile(inverse_root(var_ref[...]))


def load_kernel(after_ref, *refs):
    del after_ref
    *refs, sems = refs
    half = len(refs) // 2
    size = refs[0].shape[0] // (sems.shape[0] - half + 1)
    copies = []
    for r in range(0, refs[0].shape[0], size):
        at = pl.ds(r, size)
        copies.append(pltpu.make_async_copy(refs[0].at[at], refs[half].at[at], sems.at[len(copies)]))
    for i in range(1, half):
        copies.append(pltpu.make_async_copy(refs[i], refs[half + i], sems.at[len(copies)]))
    wait_all(start_all(copies))


class Stream:
    def __init__(self, copies, ahead=3):
        self.copies, self.ahead, self.done = copies, ahead, 0
        start_all(copies[:ahead])

    def need(self, count):
        while self.done < count:
            self.copies[self.done].wait()
            start_all(self.copies[self.done + self.ahead : self.done + self.ahead + 1])
            self.done += 1


def counts_by_cells(counts_hbm, held, sems):
    copies = []
    for b in range(held.shape[0] // COPY_CELLS):
        at = pl.ds(b * COPY_CELLS, COPY_CELLS)
        copies.append(pltpu.make_async_copy(counts_hbm.at[at], held.at[at], sems.at[b]))
    return Stream(copies)


def first_kernel(
    tile_ref, donors_hbm, table_hbm, f_hbm, l_hbm, lv_hbm, counts_hbm, ga_ref, gb_ref, off_ref, narrow_hbm,
    held, narrow, donors_ref, table_ref, f_ref, l_ref, lv_ref, load_cat, load_hl, sems, small, out_sems, *, genes_total
):
    del tile_ref
    pairs = [(l_hbm, l_ref), (f_hbm, f_ref), (donors_hbm, donors_ref), (table_hbm, table_ref), (lv_hbm, lv_ref)]
    copies = start_all([pltpu.make_async_copy(src, dst, small.at[i]) for i, (src, dst) in enumerate(pairs)])
    stream = counts_by_cells(counts_hbm, held, sems)
    wait_all(copies)
    off_ref[...] = offsets_of(donors_ref[...], table_ref[...])
    set_loads(l_ref[...], load_cat, load_hl)
    ga_ref[ga_ref.shape[0] - SUB :, :] = square_tile(inverse_root(lv_ref[...]))
    kept = []

    def ready(b):
        stream.need((b + 1) * CELL_BLOCK // COPY_CELLS)
        at = pl.ds(b * CELL_BLOCK, CELL_BLOCK)
        narrow[b] = held[at, :].astype(bf16)
        kept.append(pltpu.make_async_copy(narrow.at[b], narrow_hbm.at[at], out_sems.at[b]))
        kept[-1].start()

    cell_pass(f_ref, off_ref, load_cat, load_hl, held, ready, (ga_ref, gb_ref), genes_total)
    wait_all(kept)


def out_copies(moved, outs, sems):
    return [pltpu.make_async_copy(moved.at[i], out, sems.at[i]) for i, out in enumerate(outs)]


def gene_kernel(
    tile_ref, ga_ref, gb_ref, off_ref, counts, f_ref, fm_ref, fv_ref, l_ref,
    la_ref, lb_ref, nf_hbm, nm_hbm, nv_hbm, moved, cell_cat, cell_hl, sems, *, cells_total
):
    held = f_ref, fm_ref, fv_ref
    width, cells = moved.shape[1:]
    half = cells // LANES // 2
    tile = move(
        held, lambda c: (ga_ref if c < half else gb_ref)[c % half * width : (c % half + 1) * width, :],
        jnp.sum(tile_ref[...]), cells_total * width, rate_factors, moved,
    )
    copies = start_all(out_copies(moved, (nf_hbm, nm_hbm, nv_hbm), sems))
    rows = la_ref.shape[1]
    for h in range(2):
        la_ref[h, rows - SUB : rows, :] = tile
    set_cells(moved[0], off_ref[...], cell_cat, cell_hl)
    gene_pass(l_ref, cell_cat, cell_hl, counts, (la_ref, lb_ref), cells_total)
    wait_all(copies)


def loading_rows(la_ref, lb_ref, width, genes):
    per = genes // LANES // 4

    def grad_row(c):
        q = c // per
        return (la_ref, lb_ref)[q // 2][q % 2, c % per * width : (c % per + 1) * width, :]

    return grad_row


def cell_kernel(
    tile_ref, la_ref, lb_ref, off_ref, counts, l_ref, lm_ref, lv_ref, f_ref,
    ga_ref, gb_ref, nl_hbm, nm_hbm, nv_hbm, moved, load_cat, load_hl, sems, *, genes_total
):
    held = l_ref, lm_ref, lv_ref
    width, genes = moved.shape[1:]
    tile = move(
        held, loading_rows(la_ref, lb_ref, width, genes), jnp.sum(tile_ref[...]), genes_total * width, rate_loadings, moved
    )
    copies = start_all(out_copies(moved, (nl_hbm, nm_hbm, nv_hbm), sems))
    ga_ref[ga_ref.shape[0] - SUB :, :] = tile
    set_loads(moved[0], load_cat, load_hl)
    cell_pass(f_ref, off_ref, load_cat, load_hl, counts, None, (ga_ref, gb_ref), genes_total)
    wait_all(copies)


def last_kernel(
    tile_ref, la_ref, lb_ref, l_ref, lm_ref, lv_ref, nl_hbm, nm_hbm, nv_hbm, moved, sems, *, genes_total
):
    held = l_ref, lm_ref, lv_ref
    width, genes = moved.shape[1:]
    move(
        held, loading_rows(la_ref, lb_ref, width, genes), jnp.sum(tile_ref[...]), genes_total * width, rate_loadings, moved
    )
    wait_all(start_all(out_copies(moved, (nl_hbm, nm_hbm, nv_hbm), sems)))


def exchange(value, partner):
    pairs = []
    for cell in range(32):
        for z in range(4):
            x, y, core, depth = partner(cell // 8, cell // 2 % 4, cell % 2, z)
            pairs.append((cell * 4 + z, ((x * 4 + y) * 2 + core) * 4 + depth))
    return lax.ppermute(value, ("cell", "gene"), pairs)


def near(i):
    return i ^ 1


def far(i):
    return 3 - i


def other_core(value):
    return exchange(value, lambda x, y, core, z: (x, y, 1 - core, z))


def along_cells(step):
    turn = near if step % 2 == 0 else far

    def partner(x, y, core, z):
        if (step // 2 + core) % 2 == 0:
            return turn(x), y, core, z
        return x, turn(y), core, z

    return partner


def along_genes(step):
    def partner(x, y, core, z):
        return x, y, core, (near if (step + core) % 2 == 0 else far)(z)

    return partner


def sum_over_chips(values, seen=None):
    for step in range(4):
        came = [exchange(v, along_cells(step ^ i)) for i, v in enumerate(values)]
        values = [v + c for v, c in zip(values, came)]
        if seen is not None:
            seen += values
    return values


def sum_over_cores(halves):
    core = lax.axis_index("cell") % 2
    keep = lax.dynamic_index_in_dim(halves, core, 0, keepdims=False)
    give = lax.dynamic_index_in_dim(halves, 1 - core, 0, keepdims=False)
    return keep + other_core(give)


def both_halves(own):
    core = lax.axis_index("cell") % 2
    theirs = other_core(own)
    return jnp.stack([jnp.where(core == 0, own, theirs), jnp.where(core == 0, theirs, own)])


def sum_over_cells(first, second):
    seen = []
    first, second = sum_over_chips([sum_over_cores(first), sum_over_cores(second)], seen)
    return both_halves(first), both_halves(second), seen


def on_device(counts, donors, offset_table, factors, factor_mean, factor_var, loadings, loading_mean, loading_var):
    width, cells = factors.shape
    genes = loadings.shape[1]
    cells_total = float(cells * lax.axis_size("cell"))
    genes_total = float(genes * lax.axis_size("gene"))
    vmem = pl.BlockSpec(memory_space=pltpu.VMEM)
    hbm = pl.BlockSpec(memory_space=pltpu.HBM)
    like = lambda *shape: jax.ShapeDtypeStruct(shape, f32)
    cell_rows = width * cells // LANES // 2
    gene_rows = width * genes // LANES // 4
    flops = 2 * (2 * DEPTH) * cells * genes
    dma = lambda n: pltpu.SemaphoreType.DMA((n,))
    in_vmem = lambda *shape: pltpu.VMEM(shape, f32)
    operand = lambda *shape: pltpu.VMEM(shape, bf16)
    three_f, three_l = [like(width, cells)] * 3, [like(width, genes)] * 3
    cell_grad = [like(cell_rows + SUB, LANES), like(cell_rows, LANES)]
    gene_grad = [like(2, gene_rows + SUB, LANES), like(2, gene_rows, LANES)]

    def call(kernel, name, ins, in_hbm, outs, out_hbm, scratch, work, moves=0, limit=12, **static):
        return pl.pallas_call(
            functools.partial(kernel, **static),
            name=name,
            in_specs=[vmem] * len(ins) + [hbm] * len(in_hbm),
            out_specs=[vmem] * len(outs) + [hbm] * len(out_hbm),
            out_shape=[pltpu.VMEM(o.shape, o.dtype) for o in outs] + [pltpu.HBM(o.shape, o.dtype) for o in out_hbm],
            scratch_shapes=list(scratch),
            compiler_params=pltpu.CompilerParams(vmem_limit_bytes=(limit << 20) if work else 4 << 20),
            cost_estimate=pl.CostEstimate(
                flops=int(flops * work), bytes_accessed=4 * width * cells + moves, transcendentals=int(cells * genes * work)
            ),
        )(
            *(pltpu.with_memory_space_constraint(x, pltpu.VMEM) for x in ins),
            *(pltpu.with_memory_space_constraint(x, pltpu.HBM) for x in in_hbm),
        )

    def bring(after, *arrays):
        size = sum(a.size * a.dtype.itemsize for a in arrays)
        return call(
            load_kernel, "load", [after], list(arrays), [jax.ShapeDtypeStruct(a.shape, a.dtype) for a in arrays], [],
            [dma(len(arrays) + 3)], 0, size,
        )

    (fac_tile,) = call(
        total_kernel, "factor_scale_total", [], [factor_var], [like(SUB, LANES)], [],
        [in_vmem(width, cells), pltpu.SemaphoreType.DMA], 0,
    )
    fac_tile = fac_tile + other_core(fac_tile)
    donor_row, table_row = donors.reshape(1, cells), offset_table.reshape(1, -1)
    grad_a, grad_b, off, narrow = call(
        first_kernel, "cell_pass_first", [fac_tile], [donor_row, table_row, factors, loadings, loading_var, counts],
        cell_grad + [like(1, cells)], [jax.ShapeDtypeStruct((cells, genes), bf16)],
        [
            in_vmem(cells, genes), operand(cells // CELL_BLOCK, CELL_BLOCK, genes),
            pltpu.VMEM((1, cells), jnp.int32), pltpu.VMEM((1, table_row.shape[1]), jnp.int32),
            in_vmem(width, cells), in_vmem(width, genes), in_vmem(width, genes),
            operand(DEPTH, genes), operand(2 * width, genes), dma(cells // COPY_CELLS), dma(5),
            dma(cells // CELL_BLOCK),
        ],
        1, limit=36, genes_total=genes_total,
    )

    def loading_gradient(fac_tile, grad_a, grad_b, held):
        first, second, *new = call(
            gene_kernel, "gene_pass", [fac_tile, grad_a, grad_b, off, *held], [], gene_grad, three_f,
            [in_vmem(3, width, cells), operand(cells, DEPTH), operand(2 * width, cells), dma(3)], 1, cells_total=cells_total,
        )
        return first, second, new

    def factor_gradient(load_tile, grad_l, grad_m, held):
        first, second, *new = call(
            cell_kernel, "cell_pass", [load_tile, grad_l, grad_m, off, *held], [], cell_grad, three_l,
            [in_vmem(3, width, genes), operand(DEPTH, genes), operand(2 * width, genes), dma(3)], 1, genes_total=genes_total,
        )
        return first, second, new

    fac_tile = fac_tile + exchange(fac_tile, along_cells(0))
    grad_a, fac_tile = lax.optimization_barrier((grad_a, fac_tile))
    came_a, came_b = exchange(grad_a, along_genes(0)), exchange(grad_b, along_genes(1))
    fac_tile = fac_tile + exchange(fac_tile, along_cells(1))
    fac_tile, grad_a, grad_b = lax.optimization_barrier((fac_tile, grad_a + came_a, grad_b + came_b))
    came_a, came_b = exchange(grad_a, along_genes(1)), exchange(grad_b, along_genes(0))
    held = bring(grad_a, narrow, factors, factor_mean, factor_var, loadings)
    for step in (2, 3):
        fac_tile = fac_tile + exchange(fac_tile, along_cells(step))
    grad_a, grad_b = grad_a + came_a, grad_b + came_b
    load_tile = grad_a[cell_rows:]
    grad_l, grad_m, f = loading_gradient(fac_tile, grad_a, grad_b, held)
    grad_l, grad_m, seen = sum_over_cells(grad_l, grad_m)
    fac_tile = grad_l[0, gene_rows:]
    held = bring(seen[4], narrow, loadings, loading_mean, loading_var, f[0])
    grad_a, grad_b, l = factor_gradient(load_tile, grad_l, grad_m, held)
    came_a, came_b = exchange(grad_a, along_genes(0)), exchange(grad_b, along_genes(1))
    grad_a, grad_b = grad_a + came_a, grad_b + came_b
    came_a, came_b = exchange(grad_a, along_genes(1)), exchange(grad_b, along_genes(0))
    held = bring(grad_a, narrow, *f, l[0])
    grad_a, grad_b = grad_a + came_a, grad_b + came_b
    load_tile = grad_a[cell_rows:]
    grad_l, grad_m, f = loading_gradient(fac_tile, grad_a, grad_b, held)
    grad_l, grad_m, seen = sum_over_cells(grad_l, grad_m)
    held = bring(seen[0], *l)
    l = call(
        last_kernel, "loading_move", [load_tile, grad_l, grad_m, *held], [], [], three_l, [in_vmem(3, width, genes), dma(3)],
        0, genes_total=genes_total,
    )
    return (*f, *l)


def solution(mesh):
    by_cell, by_gene = P(None, "cell"), P(None, "gene")
    return jax.shard_map(
        on_device,
        mesh=mesh,
        in_specs=(P("cell", "gene"), P("cell"), P(), by_cell, by_cell, by_cell, by_gene, by_gene, by_gene),
        out_specs=(by_cell, by_cell, by_cell, by_gene, by_gene, by_gene),
        check_vma=False,
    )
```

```python
import functools
import math

import jax
import jax.numpy as jnp
from jax import lax
from jax.experimental import pallas as pl
from jax.experimental.pallas import tpu as pltpu
from jax.sharding import PartitionSpec as P

decay_first = 0.9
decay_second = 0.999
epsilon = 1e-06
rate_factors = 0.2
rate_loadings = 0.2
offset_unit = 0.125
LOG2E = math.log2(math.e)
LANES = 128
SUB = 8
DEPTH = 256
f32 = jnp.float32
bf16 = jnp.bfloat16
CELL_BLOCK = 512
GENE_BLOCK = 256
COPY_CELLS = 256
PARTS = 2
CHUNK = 512
FIRST_LOW_CHUNKS = 2
NARROW = jnp.float8_e4m3fn


def split(x):
    high = x.astype(bf16)
    return high, (x - high.astype(f32)).astype(bf16)


def inverse_root(variance):
    return 1.0 / (jnp.sqrt(variance) + epsilon)


def square_tile(scale):
    square = scale * scale
    total = None
    for r in range(0, scale.shape[0], SUB):
        for c in range(0, scale.shape[1], LANES):
            part = square[r : r + SUB, c : c + LANES]
            total = part if total is None else total + part
    return total


def cell_operand(f, off):
    high, low = split(f)
    first = off.astype(bf16).astype(f32)
    rest = off - first
    second = rest.astype(bf16).astype(f32)
    third = rest - second
    row = lax.broadcasted_iota(jnp.int32, f.shape, 0)
    extra = jnp.where(row == 0, first, jnp.where(row == 1, second, jnp.where(row == 2, third, 0.0)))
    return high, low, jnp.concatenate([high, high, low, extra.astype(bf16)], 0)


def gene_operand(l):
    high, low = split(l * LOG2E)
    row = lax.broadcasted_iota(jnp.int32, l.shape, 0)
    ones = jnp.where(row < 3, 1.0, 0.0).astype(bf16)
    return jnp.concatenate([high, low, high, ones], 0)


def offsets_of(donors, table):
    column = jnp.broadcast_to(table.astype(f32), (LANES, table.shape[1])).T[:, :1]
    which = lax.broadcasted_iota(jnp.int32, (table.shape[1], donors.shape[1]), 0)
    picked = jnp.where(which == donors, column, 0.0)
    return jnp.sum(picked, axis=0, keepdims=True) * (offset_unit * LOG2E)


def set_loads(l, load_cat, load_hl):
    load_cat[...] = gene_operand(l)
    high, low = split(l)
    load_hl[...] = jnp.concatenate([high, low], 0)


def set_cell_cat(f, off, cell_cat):
    _, _, cat = cell_operand(f, off)
    cell_cat[...] = cat.T


def set_cells(f, off, cell_cat, cell_hl):
    high, low, cat = cell_operand(f, off)
    cell_cat[...] = cat.T
    cell_hl[...] = jnp.concatenate([high, low], 0)


def lane_rows(grad):
    return jnp.concatenate([grad[:, c : c + LANES] for c in range(0, grad.shape[1], LANES)], 0)


def wait_all(copies):
    for copy in copies:
        copy.wait()


def start_all(copies):
    for copy in copies:
        copy.start()
    return copies


def cell_pass(cell_cat, load_cat, load_hl, counts, g_refs, genes_total, low_chunks):
    cells, genes = cell_cat.shape[0], load_cat.shape[1]
    width = load_hl.shape[0] // 2
    blocks = cells // CELL_BLOCK
    rows = width * CELL_BLOCK // LANES
    last = (((1,), (1,)), ((), ()))
    for b in range(blocks):
        lhs = cell_cat[b * CELL_BLOCK : (b + 1) * CELL_BLOCK, :]
        held = counts(b)

        def lin_of(g):
            return jnp.dot(lhs, load_cat[:, g : g + CHUNK], preferred_element_type=f32)

        total, small = None, None
        lin = lin_of(0)
        for g in range(0, genes, CHUNK):
            of = slice(g, g + CHUNK)
            resid = jnp.exp2(lin) - held[:, of].astype(f32)
            if low_chunks and g + CHUNK < genes:
                lin = lin_of(g + CHUNK)
            high, low = split(resid)
            part = lax.dot_general(load_hl[:, of], high, last, preferred_element_type=f32)
            total = part if total is None else total + part
            if g // CHUNK < low_chunks:
                part = lax.dot_general(load_hl[:width, of], low, last, preferred_element_type=f32)
                small = part if small is None else small + part
            if not low_chunks and g + CHUNK < genes:
                lin = lin_of(g + CHUNK)
        grad = total[:width] + total[width:]
        if low_chunks:
            grad += small
        half = blocks // 2
        g_refs[b // half][b % half * rows : (b % half + 1) * rows, :] = lane_rows(grad * (1.0 / math.sqrt(genes_total)))


def gene_pass(load_cat, cell_cat, cell_hl, counts, g_refs, cells_total):
    width, genes = cell_hl.shape[0] // 2, load_cat.shape[1]
    blocks = genes // GENE_BLOCK
    rows = width * GENE_BLOCK // LANES
    quarter = blocks // 4
    for b in range(blocks):
        at = slice(b * GENE_BLOCK, (b + 1) * GENE_BLOCK)
        load = load_cat[:, at]
        total = None
        for c in range(0, cell_cat.shape[0], CHUNK):
            of = slice(c, c + CHUNK)
            lin = jnp.dot(cell_cat[of, :], load, preferred_element_type=f32)
            resid = (jnp.exp2(lin) - counts[of, at].astype(f32)).astype(bf16)
            part = jnp.dot(cell_hl[:, of], resid, preferred_element_type=f32)
            total = part if total is None else total + part
        grad = (total[:width] + total[width:]) * (1.0 / math.sqrt(cells_total))
        q = b // quarter
        g_refs[q // 2][q % 2, b % quarter * rows : (b % quarter + 1) * rows, :] = lane_rows(grad)


def move(held, grad_row, total, entries, rate, moved):
    factor = rate / jnp.sqrt(total / entries)
    tile = None
    for c in range(0, moved.shape[2], LANES):
        at = slice(c, c + LANES)
        gradient = grad_row(c // LANES)
        var_old = held[2][:, at]
        mean = decay_first * held[1][:, at] + (1.0 - decay_first) * gradient
        var = decay_second * var_old + (1.0 - decay_second) * gradient * gradient
        moved[0, :, at] = held[0][:, at] - factor * mean * inverse_root(var_old)
        moved[1, :, at] = mean
        moved[2, :, at] = var
        part = square_tile(inverse_root(var))
        tile = part if tile is None else tile + part
    return tile


def front_kernel(
    fv_hbm, lv_hbm, l_hbm, donors_hbm, table_hbm, f_hbm, counts_hbm,
    fac_ref, load_ref, off_ref, load_cat, load_hl, cell_cat, front, fv_ref, lv_ref, l_ref, donors_ref, table_ref, f_ref, sems
):
    pairs = [
        (fv_hbm, fv_ref), (lv_hbm, lv_ref), (l_hbm, l_ref), (donors_hbm, donors_ref), (table_hbm, table_ref), (f_hbm, f_ref)
    ]
    copies = start_all([pltpu.make_async_copy(src, dst, sems.at[i]) for i, (src, dst) in enumerate(pairs)])
    size = front.shape[0] // 4
    blocks = []
    for b in range(4):
        at = pl.ds(b * size, size)
        blocks.append(pltpu.make_async_copy(counts_hbm.at[at], front.at[at], sems.at[len(pairs) + b]))
    start_all(blocks)
    copies[0].wait()
    fac_ref[...] = square_tile(inverse_root(fv_ref[...]))
    copies[1].wait()
    load_ref[...] = square_tile(inverse_root(lv_ref[...]))
    copies[2].wait()
    set_loads(l_ref[...], load_cat, load_hl)
    wait_all(copies[3:])
    off_ref[...] = offsets_of(donors_ref[...], table_ref[...])
    set_cell_cat(f_ref[...], off_ref[...], cell_cat)
    wait_all(blocks)


def start_loads(sources, places, sems):
    size = sources[0].shape[0] // 4
    copies = []
    for r in range(0, sources[0].shape[0], size):
        at = pl.ds(r, size)
        copies.append(pltpu.make_async_copy(sources[0].at[at], places[0].at[at], sems.at[len(copies)]))
    for source, place in zip(sources[1:], places[1:]):
        copies.append(pltpu.make_async_copy(source, place, sems.at[len(copies)]))
    return start_all(copies[::-1])


def load_kernel(after_ref, *refs):
    del after_ref
    *refs, sems = refs
    half = len(refs) // 2
    wait_all(start_loads(refs[:half], refs[half:], sems))


def load_for_genes_kernel(after_ref, *refs):
    del after_ref
    sources, places, (load_cat, l_ref, sems) = refs[:5], refs[5:9], refs[9:]
    copies = start_loads(sources, (*places, l_ref), sems)
    copies[0].wait()
    load_cat[...] = gene_operand(l_ref[...])
    wait_all(copies[1:])


def load_for_cells_kernel(after_ref, off_ref, *refs):
    del after_ref
    sources, places, (cell_cat, f_ref, sems) = refs[:5], refs[5:9], refs[9:]
    copies = start_loads(sources, (*places, f_ref), sems)
    copies[0].wait()
    set_cell_cat(f_ref[...], off_ref[...], cell_cat)
    wait_all(copies[1:])


class Stream:
    def __init__(self, copies, ahead=3):
        self.copies, self.ahead, self.done = copies, ahead, 0
        start_all(copies[:ahead])

    def need(self, count):
        while self.done < count:
            self.copies[self.done].wait()
            start_all(self.copies[self.done + self.ahead : self.done + self.ahead + 1])
            self.done += 1


def first_kernel(
    after_ref, tile_ref, load_cat, load_hl, cell_cat, front, counts_hbm, ga_ref, gb_ref, narrow_hbm,
    held, narrow, sems, out_sems, *, genes_total
):
    del after_ref
    begin = front.shape[0]
    copies = []
    for r in range(0, held.shape[0], COPY_CELLS):
        copies.append(
            pltpu.make_async_copy(
                counts_hbm.at[pl.ds(begin + r, COPY_CELLS)], held.at[pl.ds(r, COPY_CELLS)], sems.at[r // COPY_CELLS]
            )
        )
    stream = Stream(copies)
    ga_ref[ga_ref.shape[0] - SUB :, :] = tile_ref[...]
    kept = []

    def block(b):
        place = front if b == 0 else held.at[pl.ds(b * CELL_BLOCK - begin, CELL_BLOCK)]
        if len(kept) == b:
            stream.need(max(0, (b + 1) * CELL_BLOCK - begin) // COPY_CELLS)
            narrow[b] = place[...].astype(NARROW)
            kept.append(
                pltpu.make_async_copy(narrow.at[b], narrow_hbm.at[pl.ds(b * CELL_BLOCK, CELL_BLOCK)], out_sems.at[b])
            )
            kept[-1].start()
        return place

    cell_pass(cell_cat, load_cat, load_hl, block, (ga_ref, gb_ref), genes_total, FIRST_LOW_CHUNKS)
    wait_all(kept)


def out_copies(moved, outs, sems):
    return [pltpu.make_async_copy(moved.at[i], out, sems.at[i]) for i, out in enumerate(outs)]


def gene_kernel(
    tile_ref, ga_ref, gb_ref, off_ref, counts, f_ref, fm_ref, fv_ref, load_cat,
    la_ref, lb_ref, nf_hbm, nm_hbm, nv_hbm, moved, cell_cat, cell_hl, sems, *, cells_total
):
    held = f_ref, fm_ref, fv_ref
    width, cells = moved.shape[1:]
    half = cells // LANES // 2
    tile = move(
        held, lambda c: (ga_ref if c < half else gb_ref)[c % half * width : (c % half + 1) * width, :],
        jnp.sum(tile_ref[...]), cells_total * width, rate_factors, moved,
    )
    copies = start_all(out_copies(moved, (nf_hbm, nm_hbm, nv_hbm), sems))
    rows = la_ref.shape[1]
    for h in range(2):
        la_ref[h, rows - SUB : rows, :] = tile
    set_cells(moved[0], off_ref[...], cell_cat, cell_hl)
    gene_pass(load_cat, cell_cat, cell_hl, counts, (la_ref, lb_ref), cells_total)
    wait_all(copies)


def loading_rows(la_ref, lb_ref, width, genes):
    per = genes // LANES // 4

    def grad_row(c):
        q = c // per
        return (la_ref, lb_ref)[q // 2][q % 2, c % per * width : (c % per + 1) * width, :]

    return grad_row


def cell_kernel(
    tile_ref, la_ref, lb_ref, counts, l_ref, lm_ref, lv_ref, cell_cat,
    ga_ref, gb_ref, nl_hbm, nm_hbm, nv_hbm, moved, load_cat, load_hl, sems, *, genes_total
):
    held = l_ref, lm_ref, lv_ref
    width, genes = moved.shape[1:]
    tile = move(
        held, loading_rows(la_ref, lb_ref, width, genes), jnp.sum(tile_ref[...]), genes_total * width, rate_loadings, moved
    )
    copies = start_all(out_copies(moved, (nl_hbm, nm_hbm, nv_hbm), sems))
    ga_ref[ga_ref.shape[0] - SUB :, :] = tile
    set_loads(moved[0], load_cat, load_hl)
    block = lambda b: counts.at[pl.ds(b * CELL_BLOCK, CELL_BLOCK)]
    cell_pass(cell_cat, load_cat, load_hl, block, (ga_ref, gb_ref), genes_total, 0)
    wait_all(copies)


def last_kernel(
    tile_ref, la_ref, lb_ref, l_ref, lm_ref, lv_ref, nl_hbm, nm_hbm, nv_hbm, moved, sems, *, genes_total
):
    held = l_ref, lm_ref, lv_ref
    width, genes = moved.shape[1:]
    move(
        held, loading_rows(la_ref, lb_ref, width, genes), jnp.sum(tile_ref[...]), genes_total * width, rate_loadings, moved
    )
    wait_all(start_all(out_copies(moved, (nl_hbm, nm_hbm, nv_hbm), sems)))


def exchange(value, partner):
    pairs = []
    for cell in range(32):
        for z in range(4):
            x, y, core, depth = partner(cell // 8, cell // 2 % 4, cell % 2, z)
            pairs.append((cell * 4 + z, ((x * 4 + y) * 2 + core) * 4 + depth))
    return lax.ppermute(value, ("cell", "gene"), pairs)


def near(i):
    return i ^ 1


def far(i):
    return 3 - i


def other_core(value):
    return exchange(value, lambda x, y, core, z: (x, y, 1 - core, z))


def along_cells(step):
    turn = near if step % 2 == 0 else far

    def partner(x, y, core, z):
        if (step // 2 + core) % 2 == 0:
            return turn(x), y, core, z
        return x, turn(y), core, z

    return partner


def along_genes(step):
    def partner(x, y, core, z):
        return x, y, core, (near if (step + core) % 2 == 0 else far)(z)

    return partner


def sum_over_chips(values, seen=None):
    for step in range(4):
        came = [exchange(v, along_cells(step ^ i)) for i, v in enumerate(values)]
        values = [v + c for v, c in zip(values, came)]
        if seen is not None:
            seen += values
    return values


def sum_over_cores(halves):
    core = lax.axis_index("cell") % 2
    keep = lax.dynamic_index_in_dim(halves, core, 0, keepdims=False)
    give = lax.dynamic_index_in_dim(halves, 1 - core, 0, keepdims=False)
    return keep + other_core(give)


def both_halves(own):
    core = lax.axis_index("cell") % 2
    theirs = other_core(own)
    return jnp.stack([jnp.where(core == 0, own, theirs), jnp.where(core == 0, theirs, own)])


def sum_over_cells(first, second):
    seen = []
    first, second = sum_over_chips([sum_over_cores(first), sum_over_cores(second)], seen)
    return both_halves(first), both_halves(second), seen


def on_device(counts, donors, offset_table, factors, factor_mean, factor_var, loadings, loading_mean, loading_var):
    width, cells = factors.shape
    genes = loadings.shape[1]
    cells_total = float(cells * lax.axis_size("cell"))
    genes_total = float(genes * lax.axis_size("gene"))
    vmem = pl.BlockSpec(memory_space=pltpu.VMEM)
    hbm = pl.BlockSpec(memory_space=pltpu.HBM)
    like = lambda *shape: jax.ShapeDtypeStruct(shape, f32)
    cell_rows = width * cells // LANES // 2
    gene_rows = width * genes // LANES // 4
    flops = 2 * (2 * DEPTH) * cells * genes
    dma = lambda n: pltpu.SemaphoreType.DMA((n,))
    in_vmem = lambda *shape: pltpu.VMEM(shape, f32)
    operand = lambda *shape: pltpu.VMEM(shape, bf16)
    three_f, three_l = [like(width, cells)] * 3, [like(width, genes)] * 3
    cell_grad = [like(cell_rows + SUB, LANES), like(cell_rows, LANES)]
    gene_grad = [like(2, gene_rows + SUB, LANES), like(2, gene_rows, LANES)]

    def call(kernel, name, ins, in_hbm, outs, out_hbm, scratch, work, moves=0, limit=12, **static):
        return pl.pallas_call(
            functools.partial(kernel, **static),
            name=name,
            in_specs=[vmem] * len(ins) + [hbm] * len(in_hbm),
            out_specs=[vmem] * len(outs) + [hbm] * len(out_hbm),
            out_shape=[pltpu.VMEM(o.shape, o.dtype) for o in outs] + [pltpu.HBM(o.shape, o.dtype) for o in out_hbm],
            scratch_shapes=list(scratch),
            compiler_params=pltpu.CompilerParams(vmem_limit_bytes=(limit << 20) if work else 6 << 20),
            cost_estimate=pl.CostEstimate(
                flops=int(flops * work), bytes_accessed=4 * width * cells + moves, transcendentals=int(cells * genes * work)
            ),
        )(
            *(pltpu.with_memory_space_constraint(x, pltpu.VMEM) for x in ins),
            *(pltpu.with_memory_space_constraint(x, pltpu.HBM) for x in in_hbm),
        )

    def shapes(arrays):
        return [jax.ShapeDtypeStruct(a.shape, a.dtype) for a in arrays]

    def bring_for_genes(after, *arrays):
        return call(
            load_for_genes_kernel, "load_for_genes", [after], list(arrays),
            shapes(arrays[:4]) + [jax.ShapeDtypeStruct((DEPTH, genes), bf16)], [],
            [in_vmem(width, genes), dma(8)], 0, cells * genes + 16 * width * cells,
        )

    def bring_for_cells(after, off, *arrays):
        return call(
            load_for_cells_kernel, "load_for_cells", [after, off], list(arrays),
            shapes(arrays[:4]) + [jax.ShapeDtypeStruct((cells, DEPTH), bf16)], [],
            [in_vmem(width, cells), dma(8)], 0, cells * genes + 16 * width * cells,
        )

    def bring(after, *arrays):
        return call(
            load_kernel, "load", [after], list(arrays), shapes(arrays), [], [dma(len(arrays) + 3)], 0, 12 * width * cells
        )

    donor_row, table_row = donors.reshape(1, cells), offset_table.reshape(1, -1)
    operands = [jax.ShapeDtypeStruct((DEPTH, genes), bf16), jax.ShapeDtypeStruct((2 * width, genes), bf16)]
    fac_tile, load_tile, off, *ready = call(
        front_kernel, "front", [],
        [factor_var, loading_var, loadings, donor_row, table_row, factors, counts],
        [like(SUB, LANES), like(SUB, LANES), like(1, cells), *operands, jax.ShapeDtypeStruct((cells, DEPTH), bf16), like(CELL_BLOCK, genes)], [],
        [
            in_vmem(width, cells), in_vmem(width, genes), in_vmem(width, genes),
            pltpu.VMEM((1, cells), jnp.int32), pltpu.VMEM((1, table_row.shape[1]), jnp.int32),
            in_vmem(width, cells), dma(10),
        ],
        0, 4 * CELL_BLOCK * genes,
    )
    fac_tile = fac_tile + other_core(fac_tile)
    blocks = cells // CELL_BLOCK
    rest = cells - CELL_BLOCK
    grad_a, grad_b, narrow = call(
        first_kernel, "cell_pass_first", [fac_tile, load_tile, *ready], [counts],
        cell_grad, [jax.ShapeDtypeStruct((cells, genes), NARROW)],
        [
            in_vmem(rest, genes), pltpu.VMEM((blocks, CELL_BLOCK, genes), NARROW), dma(rest // COPY_CELLS), dma(blocks),
        ],
        1.5, limit=32, genes_total=genes_total,
    )

    def loading_gradient(fac_tile, grad_a, grad_b, held):
        first, second, *new = call(
            gene_kernel, "gene_pass", [fac_tile, grad_a, grad_b, off, *held], [], gene_grad, three_f,
            [in_vmem(3, width, cells), operand(cells, DEPTH), operand(2 * width, cells), dma(3)], 1, cells_total=cells_total,
        )
        return first, second, new

    def factor_gradient(load_tile, grad_l, grad_m, held):
        first, second, *new = call(
            cell_kernel, "cell_pass", [load_tile, grad_l, grad_m, *held], [], cell_grad, three_l,
            [in_vmem(3, width, genes), operand(DEPTH, genes), operand(2 * width, genes), dma(3)], 1, genes_total=genes_total,
        )
        return first, second, new

    fac_tile = fac_tile + exchange(fac_tile, along_cells(0))
    grad_a, fac_tile = lax.optimization_barrier((grad_a, fac_tile))
    came_a, came_b = exchange(grad_a, along_genes(0)), exchange(grad_b, along_genes(0))
    fac_tile = fac_tile + exchange(fac_tile, along_cells(1))
    fac_tile, grad_a, grad_b = lax.optimization_barrier((fac_tile, grad_a + came_a, grad_b + came_b))
    came_a, came_b = exchange(grad_a, along_genes(1)), exchange(grad_b, along_genes(1))
    held = bring_for_genes(grad_a, narrow, factors, factor_mean, factor_var, loadings)
    for step in (2, 3):
        fac_tile = fac_tile + exchange(fac_tile, along_cells(step))
    grad_a, grad_b = grad_a + came_a, grad_b + came_b
    load_tile = grad_a[cell_rows:]
    grad_l, grad_m, f = loading_gradient(fac_tile, grad_a, grad_b, held)
    grad_l, grad_m, seen = sum_over_cells(grad_l, grad_m)
    fac_tile = grad_l[0, gene_rows:]
    held = bring_for_cells(seen[4], off, narrow, loadings, loading_mean, loading_var, f[0])
    grad_a, grad_b, l = factor_gradient(load_tile, grad_l, grad_m, held)
    came_a, came_b = exchange(grad_a, along_genes(0)), exchange(grad_b, along_genes(0))
    grad_a, grad_b = grad_a + came_a, grad_b + came_b
    came_a, came_b = exchange(grad_a, along_genes(1)), exchange(grad_b, along_genes(1))
    held = bring_for_genes(grad_a, narrow, *f, l[0])
    grad_a, grad_b = grad_a + came_a, grad_b + came_b
    load_tile = grad_a[cell_rows:]
    grad_l, grad_m, f = loading_gradient(fac_tile, grad_a, grad_b, held)
    grad_l, grad_m, seen = sum_over_cells(grad_l, grad_m)
    held = bring(seen[0], *l)
    l = call(
        last_kernel, "loading_move", [load_tile, grad_l, grad_m, *held], [], [], three_l, [in_vmem(3, width, genes), dma(3)],
        0, genes_total=genes_total,
    )
    return (*f, *l)


def solution(mesh):
    by_cell, by_gene = P(None, "cell"), P(None, "gene")
    return jax.shard_map(
        on_device,
        mesh=mesh,
        in_specs=(P("cell", "gene"), P("cell"), P(), by_cell, by_cell, by_cell, by_gene, by_gene, by_gene),
        out_specs=(by_cell, by_cell, by_cell, by_gene, by_gene, by_gene),
        check_vma=False,
    )
```

```python
import functools
import math

import jax
import jax.numpy as jnp
from jax import lax
from jax.experimental import pallas as pl
from jax.experimental.pallas import tpu as pltpu
from jax.sharding import PartitionSpec as P

decay_first = 0.9
decay_second = 0.999
epsilon = 1e-06
rate_factors = 0.2
rate_loadings = 0.2
offset_unit = 0.125
LOG2E = math.log2(math.e)
LANES = 128
SUB = 8
DEPTH = 256
f32 = jnp.float32
bf16 = jnp.bfloat16
CELL_BLOCK = 512
GENE_BLOCK = 256
COPY_CELLS = 256
PARTS = 2
CHUNK = 512
FIRST_LOW_CHUNKS = 2
NARROW = jnp.float8_e4m3fn


def split(x):
    high = x.astype(bf16)
    return high, (x - high.astype(f32)).astype(bf16)


def inverse_root(variance):
    return 1.0 / (jnp.sqrt(variance) + epsilon)


def square_tile(scale):
    square = scale * scale
    total = None
    for r in range(0, scale.shape[0], SUB):
        for c in range(0, scale.shape[1], LANES):
            part = square[r : r + SUB, c : c + LANES]
            total = part if total is None else total + part
    return total


def cell_operand(f, off):
    high, low = split(f)
    first = off.astype(bf16).astype(f32)
    rest = off - first
    second = rest.astype(bf16).astype(f32)
    third = rest - second
    row = lax.broadcasted_iota(jnp.int32, f.shape, 0)
    extra = jnp.where(row == 0, first, jnp.where(row == 1, second, jnp.where(row == 2, third, 0.0)))
    return high, low, jnp.concatenate([high, high, low, extra.astype(bf16)], 0)


def gene_operand(l):
    high, low = split(l * LOG2E)
    row = lax.broadcasted_iota(jnp.int32, l.shape, 0)
    ones = jnp.where(row < 3, 1.0, 0.0).astype(bf16)
    return jnp.concatenate([high, low, high, ones], 0)


def offsets_of(donors, table):
    column = jnp.broadcast_to(table.astype(f32), (LANES, table.shape[1])).T[:, :1]
    which = lax.broadcasted_iota(jnp.int32, (table.shape[1], donors.shape[1]), 0)
    picked = jnp.where(which == donors, column, 0.0)
    return jnp.sum(picked, axis=0, keepdims=True) * (offset_unit * LOG2E)


def set_loads(l, load_cat, load_hl):
    load_cat[...] = gene_operand(l)
    high, low = split(l)
    load_hl[...] = jnp.concatenate([high, low], 0)


def set_cell_cat(f, off, cell_cat):
    _, _, cat = cell_operand(f, off)
    cell_cat[...] = cat.T


def set_cells(f, off, cell_cat, cell_hl):
    high, low, cat = cell_operand(f, off)
    cell_cat[...] = cat.T
    cell_hl[...] = jnp.concatenate([high, low], 0)


def lane_rows(grad):
    return jnp.concatenate([grad[:, c : c + LANES] for c in range(0, grad.shape[1], LANES)], 0)


def wait_all(copies):
    for copy in copies:
        copy.wait()


def start_all(copies):
    for copy in copies:
        copy.start()
    return copies


def cell_pass(cell_cat, load_cat, load_hl, counts, g_refs, genes_total, low_chunks):
    cells, genes = cell_cat.shape[0], load_cat.shape[1]
    width = load_hl.shape[0] // 2
    blocks = cells // CELL_BLOCK
    rows = width * CELL_BLOCK // LANES
    last = (((1,), (1,)), ((), ()))
    for b in range(blocks):
        lhs = cell_cat[b * CELL_BLOCK : (b + 1) * CELL_BLOCK, :]
        held = counts(b)

        def lin_of(g):
            return jnp.dot(lhs, load_cat[:, g : g + CHUNK], preferred_element_type=f32)

        total, small = None, None
        lin = lin_of(0)
        for g in range(0, genes, CHUNK):
            of = slice(g, g + CHUNK)
            resid = jnp.exp2(lin) - held[:, of].astype(f32)
            if low_chunks and g + CHUNK < genes:
                lin = lin_of(g + CHUNK)
            high, low = split(resid)
            part = lax.dot_general(load_hl[:, of], high, last, preferred_element_type=f32)
            total = part if total is None else total + part
            if g // CHUNK < low_chunks:
                part = lax.dot_general(load_hl[:width, of], low, last, preferred_element_type=f32)
                small = part if small is None else small + part
            if not low_chunks and g + CHUNK < genes:
                lin = lin_of(g + CHUNK)
        grad = total[:width] + total[width:]
        if low_chunks:
            grad += small
        half = blocks // 2
        g_refs[b // half][b % half * rows : (b % half + 1) * rows, :] = lane_rows(grad * (1.0 / math.sqrt(genes_total)))


def gene_pass(load_cat, cell_cat, cell_hl, counts, g_refs, cells_total):
    width, genes = cell_hl.shape[0] // 2, load_cat.shape[1]
    blocks = genes // GENE_BLOCK
    rows = width * GENE_BLOCK // LANES
    quarter = blocks // 4
    for b in range(blocks):
        at = slice(b * GENE_BLOCK, (b + 1) * GENE_BLOCK)
        load = load_cat[:, at]
        total = None
        for c in range(0, cell_cat.shape[0], CHUNK):
            of = slice(c, c + CHUNK)
            lin = jnp.dot(cell_cat[of, :], load, preferred_element_type=f32)
            resid = (jnp.exp2(lin) - counts[of, at].astype(f32)).astype(bf16)
            part = jnp.dot(cell_hl[:, of], resid, preferred_element_type=f32)
            total = part if total is None else total + part
        grad = (total[:width] + total[width:]) * (1.0 / math.sqrt(cells_total))
        q = b // quarter
        g_refs[q // 2][q % 2, b % quarter * rows : (b % quarter + 1) * rows, :] = lane_rows(grad)


def move(held, grad_row, total, entries, rate, moved):
    factor = rate / jnp.sqrt(total / entries)
    tile = None
    for c in range(0, moved.shape[2], LANES):
        at = slice(c, c + LANES)
        gradient = grad_row(c // LANES)
        var_old = held[2][:, at]
        mean = decay_first * held[1][:, at] + (1.0 - decay_first) * gradient
        var = decay_second * var_old + (1.0 - decay_second) * gradient * gradient
        moved[0, :, at] = held[0][:, at] - factor * mean * inverse_root(var_old)
        moved[1, :, at] = mean
        moved[2, :, at] = var
        part = square_tile(inverse_root(var))
        tile = part if tile is None else tile + part
    return tile


def front_kernel(
    fv_hbm, lv_hbm, l_hbm, donors_hbm, table_hbm, f_hbm, counts_hbm,
    fac_ref, load_ref, off_ref, load_cat, load_hl, cell_cat, front, fv_ref, lv_ref, l_ref, donors_ref, table_ref, f_ref, sems
):
    pairs = [
        (fv_hbm, fv_ref), (lv_hbm, lv_ref), (l_hbm, l_ref), (donors_hbm, donors_ref), (table_hbm, table_ref), (f_hbm, f_ref)
    ]
    copies = start_all([pltpu.make_async_copy(src, dst, sems.at[i]) for i, (src, dst) in enumerate(pairs)])
    size = front.shape[0] // 4
    blocks = []
    for b in range(4):
        at = pl.ds(b * size, size)
        blocks.append(pltpu.make_async_copy(counts_hbm.at[at], front.at[at], sems.at[len(pairs) + b]))
    start_all(blocks)
    copies[0].wait()
    fac_ref[...] = square_tile(inverse_root(fv_ref[...]))
    copies[1].wait()
    load_ref[...] = square_tile(inverse_root(lv_ref[...]))
    copies[2].wait()
    set_loads(l_ref[...], load_cat, load_hl)
    wait_all(copies[3:])
    off_ref[...] = offsets_of(donors_ref[...], table_ref[...])
    set_cell_cat(f_ref[...], off_ref[...], cell_cat)
    wait_all(blocks)


def start_loads(sources, places, sems):
    size = sources[0].shape[0] // 4
    copies = []
    for r in range(0, sources[0].shape[0], size):
        at = pl.ds(r, size)
        copies.append(pltpu.make_async_copy(sources[0].at[at], places[0].at[at], sems.at[len(copies)]))
    for source, place in zip(sources[1:], places[1:]):
        copies.append(pltpu.make_async_copy(source, place, sems.at[len(copies)]))
    return start_all(copies[::-1])


def load_kernel(after_ref, *refs):
    del after_ref
    *refs, sems = refs
    half = len(refs) // 2
    wait_all(start_loads(refs[:half], refs[half:], sems))


def load_for_genes_kernel(after_ref, *refs):
    del after_ref
    sources, places, (load_cat, l_ref, sems) = refs[:5], refs[5:9], refs[9:]
    copies = start_loads(sources, (*places, l_ref), sems)
    copies[0].wait()
    load_cat[...] = gene_operand(l_ref[...])
    wait_all(copies[1:])


def load_for_cells_kernel(after_ref, off_ref, *refs):
    del after_ref
    sources, places, (cell_cat, f_ref, sems) = refs[:5], refs[5:9], refs[9:]
    copies = start_loads(sources, (*places, f_ref), sems)
    copies[0].wait()
    set_cell_cat(f_ref[...], off_ref[...], cell_cat)
    wait_all(copies[1:])


class Stream:
    def __init__(self, copies, ahead=3):
        self.copies, self.ahead, self.done = copies, ahead, 0
        start_all(copies[:ahead])

    def need(self, count):
        while self.done < count:
            self.copies[self.done].wait()
            start_all(self.copies[self.done + self.ahead : self.done + self.ahead + 1])
            self.done += 1


def first_kernel(
    after_ref, tile_ref, load_cat, load_hl, cell_cat, front, counts_hbm, ga_ref, gb_ref, narrow_hbm,
    held, narrow, sems, out_sems, *, genes_total
):
    del after_ref
    begin = front.shape[0]
    copies = []
    for r in range(0, held.shape[0], COPY_CELLS):
        copies.append(
            pltpu.make_async_copy(
                counts_hbm.at[pl.ds(begin + r, COPY_CELLS)], held.at[pl.ds(r, COPY_CELLS)], sems.at[r // COPY_CELLS]
            )
        )
    stream = Stream(copies)
    ga_ref[ga_ref.shape[0] - SUB :, :] = tile_ref[...]
    kept = []

    def block(b):
        place = front if b == 0 else held.at[pl.ds(b * CELL_BLOCK - begin, CELL_BLOCK)]
        if len(kept) == b:
            stream.need(max(0, (b + 1) * CELL_BLOCK - begin) // COPY_CELLS)
            narrow[b] = place[...].astype(NARROW)
            kept.append(
                pltpu.make_async_copy(narrow.at[b], narrow_hbm.at[pl.ds(b * CELL_BLOCK, CELL_BLOCK)], out_sems.at[b])
            )
            kept[-1].start()
        return place

    cell_pass(cell_cat, load_cat, load_hl, block, (ga_ref, gb_ref), genes_total, FIRST_LOW_CHUNKS)
    wait_all(kept)


def out_copies(moved, outs, sems):
    return [pltpu.make_async_copy(moved.at[i], out, sems.at[i]) for i, out in enumerate(outs)]


def gene_kernel(
    tile_ref, ga_ref, gb_ref, off_ref, counts, f_ref, fm_ref, fv_ref, load_cat,
    la_ref, lb_ref, nf_hbm, nm_hbm, nv_hbm, moved, cell_cat, cell_hl, sems, *, cells_total
):
    held = f_ref, fm_ref, fv_ref
    width, cells = moved.shape[1:]
    half = cells // LANES // 2
    tile = move(
        held, lambda c: (ga_ref if c < half else gb_ref)[c % half * width : (c % half + 1) * width, :],
        jnp.sum(tile_ref[...]), cells_total * width, rate_factors, moved,
    )
    copies = start_all(out_copies(moved, (nf_hbm, nm_hbm, nv_hbm), sems))
    rows = la_ref.shape[1]
    for h in range(2):
        la_ref[h, rows - SUB : rows, :] = tile
    set_cells(moved[0], off_ref[...], cell_cat, cell_hl)
    gene_pass(load_cat, cell_cat, cell_hl, counts, (la_ref, lb_ref), cells_total)
    wait_all(copies)


def loading_rows(la_ref, lb_ref, width, genes):
    per = genes // LANES // 4

    def grad_row(c):
        q = c // per
        return (la_ref, lb_ref)[q // 2][q % 2, c % per * width : (c % per + 1) * width, :]

    return grad_row


def cell_kernel(
    tile_ref, la_ref, lb_ref, counts, l_ref, lm_ref, lv_ref, cell_cat,
    ga_ref, gb_ref, nl_hbm, nm_hbm, nv_hbm, moved, load_cat, load_hl, sems, *, genes_total
):
    held = l_ref, lm_ref, lv_ref
    width, genes = moved.shape[1:]
    tile = move(
        held, loading_rows(la_ref, lb_ref, width, genes), jnp.sum(tile_ref[...]), genes_total * width, rate_loadings, moved
    )
    copies = start_all(out_copies(moved, (nl_hbm, nm_hbm, nv_hbm), sems))
    ga_ref[ga_ref.shape[0] - SUB :, :] = tile
    set_loads(moved[0], load_cat, load_hl)
    block = lambda b: counts.at[pl.ds(b * CELL_BLOCK, CELL_BLOCK)]
    cell_pass(cell_cat, load_cat, load_hl, block, (ga_ref, gb_ref), genes_total, 0)
    wait_all(copies)


def last_kernel(
    tile_ref, la_ref, lb_ref, l_ref, lm_ref, lv_ref, nl_hbm, nm_hbm, nv_hbm, moved, sems, *, genes_total
):
    held = l_ref, lm_ref, lv_ref
    width, genes = moved.shape[1:]
    move(
        held, loading_rows(la_ref, lb_ref, width, genes), jnp.sum(tile_ref[...]), genes_total * width, rate_loadings, moved
    )
    wait_all(start_all(out_copies(moved, (nl_hbm, nm_hbm, nv_hbm), sems)))


def exchange(value, partner):
    pairs = []
    for cell in range(32):
        for z in range(4):
            x, y, core, depth = partner(cell // 8, cell // 2 % 4, cell % 2, z)
            pairs.append((cell * 4 + z, ((x * 4 + y) * 2 + core) * 4 + depth))
    return lax.ppermute(value, ("cell", "gene"), pairs)


def near(i):
    return i ^ 1


def far(i):
    return 3 - i


def other_core(value):
    return exchange(value, lambda x, y, core, z: (x, y, 1 - core, z))


def along_cells(step):
    turn = near if step % 2 == 0 else far

    def partner(x, y, core, z):
        if (step // 2 + core) % 2 == 0:
            return turn(x), y, core, z
        return x, turn(y), core, z

    return partner


def along_genes(step):
    def partner(x, y, core, z):
        return x, y, core, (near if (step + core) % 2 == 0 else far)(z)

    return partner


def sum_over_chips(values, seen=None):
    for step in range(4):
        came = [exchange(v, along_cells(step ^ i)) for i, v in enumerate(values)]
        values = [v + c for v, c in zip(values, came)]
        if seen is not None:
            seen += values
    return values


def sum_over_cores(halves):
    core = lax.axis_index("cell") % 2
    keep = lax.dynamic_index_in_dim(halves, core, 0, keepdims=False)
    give = lax.dynamic_index_in_dim(halves, 1 - core, 0, keepdims=False)
    return keep + other_core(give)


def both_halves(own):
    core = lax.axis_index("cell") % 2
    theirs = other_core(own)
    return jnp.stack([jnp.where(core == 0, own, theirs), jnp.where(core == 0, theirs, own)])


def sum_over_cells(first, second):
    seen = []
    first, second = sum_over_chips([sum_over_cores(first), sum_over_cores(second)], seen)
    return both_halves(first), both_halves(second), seen


def on_device(counts, donors, offset_table, factors, factor_mean, factor_var, loadings, loading_mean, loading_var):
    width, cells = factors.shape
    genes = loadings.shape[1]
    cells_total = float(cells * lax.axis_size("cell"))
    genes_total = float(genes * lax.axis_size("gene"))
    vmem = pl.BlockSpec(memory_space=pltpu.VMEM)
    hbm = pl.BlockSpec(memory_space=pltpu.HBM)
    like = lambda *shape: jax.ShapeDtypeStruct(shape, f32)
    cell_rows = width * cells // LANES // 2
    gene_rows = width * genes // LANES // 4
    flops = 2 * (2 * DEPTH) * cells * genes
    dma = lambda n: pltpu.SemaphoreType.DMA((n,))
    in_vmem = lambda *shape: pltpu.VMEM(shape, f32)
    operand = lambda *shape: pltpu.VMEM(shape, bf16)
    three_f, three_l = [like(width, cells)] * 3, [like(width, genes)] * 3
    cell_grad = [like(cell_rows + SUB, LANES), like(cell_rows, LANES)]
    gene_grad = [like(2, gene_rows + SUB, LANES), like(2, gene_rows, LANES)]

    def call(kernel, name, ins, in_hbm, outs, out_hbm, scratch, work, moves=0, limit=12, **static):
        return pl.pallas_call(
            functools.partial(kernel, **static),
            name=name,
            in_specs=[vmem] * len(ins) + [hbm] * len(in_hbm),
            out_specs=[vmem] * len(outs) + [hbm] * len(out_hbm),
            out_shape=[pltpu.VMEM(o.shape, o.dtype) for o in outs] + [pltpu.HBM(o.shape, o.dtype) for o in out_hbm],
            scratch_shapes=list(scratch),
            compiler_params=pltpu.CompilerParams(vmem_limit_bytes=(limit << 20) if work else 6 << 20),
            cost_estimate=pl.CostEstimate(
                flops=int(flops * work), bytes_accessed=4 * width * cells + moves, transcendentals=int(cells * genes * work)
            ),
        )(
            *(pltpu.with_memory_space_constraint(x, pltpu.VMEM) for x in ins),
            *(pltpu.with_memory_space_constraint(x, pltpu.HBM) for x in in_hbm),
        )

    def shapes(arrays):
        return [jax.ShapeDtypeStruct(a.shape, a.dtype) for a in arrays]

    def bring_for_genes(after, *arrays):
        return call(
            load_for_genes_kernel, "load_for_genes", [after], list(arrays),
            shapes(arrays[:4]) + [jax.ShapeDtypeStruct((DEPTH, genes), bf16)], [],
            [in_vmem(width, genes), dma(8)], 0, cells * genes + 16 * width * cells,
        )

    def bring_for_cells(after, off, *arrays):
        return call(
            load_for_cells_kernel, "load_for_cells", [after, off], list(arrays),
            shapes(arrays[:4]) + [jax.ShapeDtypeStruct((cells, DEPTH), bf16)], [],
            [in_vmem(width, cells), dma(8)], 0, cells * genes + 16 * width * cells,
        )

    def bring(after, *arrays):
        return call(
            load_kernel, "load", [after], list(arrays), shapes(arrays), [], [dma(len(arrays) + 3)], 0, 12 * width * cells
        )

    donor_row, table_row = donors.reshape(1, cells), offset_table.reshape(1, -1)
    operands = [jax.ShapeDtypeStruct((DEPTH, genes), bf16), jax.ShapeDtypeStruct((2 * width, genes), bf16)]
    fac_tile, load_tile, off, *ready = call(
        front_kernel, "front", [],
        [factor_var, loading_var, loadings, donor_row, table_row, factors, counts],
        [like(SUB, LANES), like(SUB, LANES), like(1, cells), *operands, jax.ShapeDtypeStruct((cells, DEPTH), bf16), like(CELL_BLOCK, genes)], [],
        [
            in_vmem(width, cells), in_vmem(width, genes), in_vmem(width, genes),
            pltpu.VMEM((1, cells), jnp.int32), pltpu.VMEM((1, table_row.shape[1]), jnp.int32),
            in_vmem(width, cells), dma(10),
        ],
        0, 4 * CELL_BLOCK * genes,
    )
    fac_tile = fac_tile + other_core(fac_tile)
    blocks = cells // CELL_BLOCK
    rest = cells - CELL_BLOCK
    grad_a, grad_b, narrow = call(
        first_kernel, "cell_pass_first", [fac_tile, load_tile, *ready], [counts],
        cell_grad, [jax.ShapeDtypeStruct((cells, genes), NARROW)],
        [
            in_vmem(rest, genes), pltpu.VMEM((blocks, CELL_BLOCK, genes), NARROW), dma(rest // COPY_CELLS), dma(blocks),
        ],
        1.5, limit=32, genes_total=genes_total,
    )

    def loading_gradient(fac_tile, grad_a, grad_b, held):
        first, second, *new = call(
            gene_kernel, "gene_pass", [fac_tile, grad_a, grad_b, off, *held], [], gene_grad, three_f,
            [in_vmem(3, width, cells), operand(cells, DEPTH), operand(2 * width, cells), dma(3)], 1, cells_total=cells_total,
        )
        return first, second, new

    def factor_gradient(load_tile, grad_l, grad_m, held):
        first, second, *new = call(
            cell_kernel, "cell_pass", [load_tile, grad_l, grad_m, *held], [], cell_grad, three_l,
            [in_vmem(3, width, genes), operand(DEPTH, genes), operand(2 * width, genes), dma(3)], 1, genes_total=genes_total,
        )
        return first, second, new

    fac_tile = fac_tile + exchange(fac_tile, along_cells(0))
    grad_a, fac_tile = lax.optimization_barrier((grad_a, fac_tile))
    came_a, came_b = exchange(grad_a, along_genes(0)), exchange(grad_b, along_genes(0))
    for step in (1, 2):
        fac_tile = fac_tile + exchange(fac_tile, along_cells(step))
    fac_tile, grad_a, grad_b = lax.optimization_barrier((fac_tile, grad_a + came_a, grad_b + came_b))
    came_a, came_b = exchange(grad_a, along_genes(1)), exchange(grad_b, along_genes(1))
    held = bring_for_genes(grad_a, narrow, factors, factor_mean, factor_var, loadings)
    fac_tile = fac_tile + exchange(fac_tile, along_cells(3))
    grad_a, grad_b = grad_a + came_a, grad_b + came_b
    load_tile = grad_a[cell_rows:]
    grad_l, grad_m, f = loading_gradient(fac_tile, grad_a, grad_b, held)
    grad_l, grad_m, seen = sum_over_cells(grad_l, grad_m)
    fac_tile = grad_l[0, gene_rows:]
    held = bring_for_cells(seen[4], off, narrow, loadings, loading_mean, loading_var, f[0])
    grad_a, grad_b, l = factor_gradient(load_tile, grad_l, grad_m, held)
    came_a, came_b = exchange(grad_a, along_genes(0)), exchange(grad_b, along_genes(0))
    grad_a, grad_b = grad_a + came_a, grad_b + came_b
    came_a, came_b = exchange(grad_a, along_genes(1)), exchange(grad_b, along_genes(1))
    held = bring_for_genes(grad_a, narrow, *f, l[0])
    grad_a, grad_b = grad_a + came_a, grad_b + came_b
    load_tile = grad_a[cell_rows:]
    grad_l, grad_m, f = loading_gradient(fac_tile, grad_a, grad_b, held)
    grad_l, grad_m, seen = sum_over_cells(grad_l, grad_m)
    held = bring(seen[0], *l)
    l = call(
        last_kernel, "loading_move", [load_tile, grad_l, grad_m, *held], [], [], three_l, [in_vmem(3, width, genes), dma(3)],
        0, genes_total=genes_total,
    )
    return (*f, *l)


def solution(mesh):
    by_cell, by_gene = P(None, "cell"), P(None, "gene")
    return jax.shard_map(
        on_device,
        mesh=mesh,
        in_specs=(P("cell", "gene"), P("cell"), P(), by_cell, by_cell, by_cell, by_gene, by_gene, by_gene),
        out_specs=(by_cell, by_cell, by_cell, by_gene, by_gene, by_gene),
        check_vma=False,
    )
```

```python
import functools
import math

import jax
import jax.numpy as jnp
from jax import lax
from jax.experimental import pallas as pl
from jax.experimental.pallas import tpu as pltpu
from jax.sharding import PartitionSpec as P

decay_first = 0.9
decay_second = 0.999
epsilon = 1e-06
rate_factors = 0.2
rate_loadings = 0.2
offset_unit = 0.125
LOG2E = math.log2(math.e)
LANES = 128
SUB = 8
DEPTH = 256
f32 = jnp.float32
bf16 = jnp.bfloat16
CELL_BLOCK = 512
GENE_BLOCK = 256
COPY_CELLS = 256
PARTS = 2
CHUNK = 512
FIRST_LOW_CHUNKS = 2
NARROW = jnp.float8_e4m3fn


def split(x):
    high = x.astype(bf16)
    return high, (x - high.astype(f32)).astype(bf16)


def inverse_root(variance):
    return 1.0 / (jnp.sqrt(variance) + epsilon)


def square_tile(scale):
    square = scale * scale
    total = None
    for r in range(0, scale.shape[0], SUB):
        for c in range(0, scale.shape[1], LANES):
            part = square[r : r + SUB, c : c + LANES]
            total = part if total is None else total + part
    return total


def cell_operand(f, off):
    high, low = split(f)
    first = off.astype(bf16).astype(f32)
    rest = off - first
    second = rest.astype(bf16).astype(f32)
    third = rest - second
    row = lax.broadcasted_iota(jnp.int32, f.shape, 0)
    extra = jnp.where(row == 0, first, jnp.where(row == 1, second, jnp.where(row == 2, third, 0.0)))
    return high, low, jnp.concatenate([high, high, low, extra.astype(bf16)], 0)


def gene_operand(l):
    high, low = split(l * LOG2E)
    row = lax.broadcasted_iota(jnp.int32, l.shape, 0)
    ones = jnp.where(row < 3, 1.0, 0.0).astype(bf16)
    return jnp.concatenate([high, low, high, ones], 0)


def offsets_of(donors, table):
    column = jnp.broadcast_to(table.astype(f32), (LANES, table.shape[1])).T[:, :1]
    which = lax.broadcasted_iota(jnp.int32, (table.shape[1], donors.shape[1]), 0)
    picked = jnp.where(which == donors, column, 0.0)
    return jnp.sum(picked, axis=0, keepdims=True) * (offset_unit * LOG2E)


def set_loads(l, load_cat, load_hl):
    load_cat[...] = gene_operand(l)
    high, low = split(l)
    load_hl[...] = jnp.concatenate([high, low], 0)


def set_cell_cat(f, off, cell_cat):
    _, _, cat = cell_operand(f, off)
    cell_cat[...] = cat.T


def set_cells(f, off, cell_cat, cell_hl):
    high, low, cat = cell_operand(f, off)
    cell_cat[...] = cat.T
    cell_hl[...] = jnp.concatenate([high, low], 0)


def lane_rows(grad):
    return jnp.concatenate([grad[:, c : c + LANES] for c in range(0, grad.shape[1], LANES)], 0)


def wait_all(copies):
    for copy in copies:
        copy.wait()


def start_all(copies):
    for copy in copies:
        copy.start()
    return copies


def cell_pass(cell_cat, load_cat, load_hl, counts, g_refs, genes_total, low_chunks):
    cells, genes = cell_cat.shape[0], load_cat.shape[1]
    width = load_hl.shape[0] // 2
    blocks = cells // CELL_BLOCK
    rows = width * CELL_BLOCK // LANES
    last = (((1,), (1,)), ((), ()))
    for b in range(blocks):
        lhs = cell_cat[b * CELL_BLOCK : (b + 1) * CELL_BLOCK, :]
        held = counts(b)

        def lin_of(g):
            return jnp.dot(lhs, load_cat[:, g : g + CHUNK], preferred_element_type=f32)

        total, small = None, None
        lin = lin_of(0)
        for g in range(0, genes, CHUNK):
            of = slice(g, g + CHUNK)
            resid = jnp.exp2(lin) - held[:, of].astype(f32)
            if low_chunks and g + CHUNK < genes:
                lin = lin_of(g + CHUNK)
            high, low = split(resid)
            part = lax.dot_general(load_hl[:, of], high, last, preferred_element_type=f32)
            total = part if total is None else total + part
            if g // CHUNK < low_chunks:
                part = lax.dot_general(load_hl[:width, of], low, last, preferred_element_type=f32)
                small = part if small is None else small + part
            if not low_chunks and g + CHUNK < genes:
                lin = lin_of(g + CHUNK)
        grad = total[:width] + total[width:]
        if low_chunks:
            grad += small
        half = blocks // 2
        g_refs[b // half][b % half * rows : (b % half + 1) * rows, :] = lane_rows(grad * (1.0 / math.sqrt(genes_total)))


def gene_pass(load_cat, cell_cat, cell_hl, counts, g_refs, cells_total):
    width, genes = cell_hl.shape[0] // 2, load_cat.shape[1]
    blocks = genes // GENE_BLOCK
    rows = width * GENE_BLOCK // LANES
    quarter = blocks // 4
    for b in range(blocks):
        at = slice(b * GENE_BLOCK, (b + 1) * GENE_BLOCK)
        load = load_cat[:, at]
        total = None
        for c in range(0, cell_cat.shape[0], CHUNK):
            of = slice(c, c + CHUNK)
            lin = jnp.dot(cell_cat[of, :], load, preferred_element_type=f32)
            resid = (jnp.exp2(lin) - counts[of, at].astype(f32)).astype(bf16)
            part = jnp.dot(cell_hl[:, of], resid, preferred_element_type=f32)
            total = part if total is None else total + part
        grad = (total[:width] + total[width:]) * (1.0 / math.sqrt(cells_total))
        q = b // quarter
        g_refs[q // 2][q % 2, b % quarter * rows : (b % quarter + 1) * rows, :] = lane_rows(grad)


def move(held, grad_row, total, entries, rate, moved):
    factor = rate / jnp.sqrt(total / entries)
    tile = None
    for c in range(0, moved.shape[2], LANES):
        at = slice(c, c + LANES)
        gradient = grad_row(c // LANES)
        var_old = held[2][:, at]
        mean = decay_first * held[1][:, at] + (1.0 - decay_first) * gradient
        var = decay_second * var_old + (1.0 - decay_second) * gradient * gradient
        moved[0, :, at] = held[0][:, at] - factor * mean * inverse_root(var_old)
        moved[1, :, at] = mean
        moved[2, :, at] = var
        part = square_tile(inverse_root(var))
        tile = part if tile is None else tile + part
    return tile


def front_kernel(
    fv_hbm, lv_hbm, l_hbm, donors_hbm, table_hbm, f_hbm, counts_hbm,
    fac_ref, load_ref, off_ref, load_cat, load_hl, cell_cat, front, fv_ref, lv_ref, l_ref, donors_ref, table_ref, f_ref, sems
):
    pairs = [
        (fv_hbm, fv_ref), (lv_hbm, lv_ref), (l_hbm, l_ref), (donors_hbm, donors_ref), (table_hbm, table_ref), (f_hbm, f_ref)
    ]
    copies = start_all([pltpu.make_async_copy(src, dst, sems.at[i]) for i, (src, dst) in enumerate(pairs)])
    size = front.shape[0] // 4
    blocks = []
    for b in range(4):
        at = pl.ds(b * size, size)
        blocks.append(pltpu.make_async_copy(counts_hbm.at[at], front.at[at], sems.at[len(pairs) + b]))
    start_all(blocks)
    copies[0].wait()
    fac_ref[...] = square_tile(inverse_root(fv_ref[...]))
    copies[1].wait()
    load_ref[...] = square_tile(inverse_root(lv_ref[...]))
    copies[2].wait()
    set_loads(l_ref[...], load_cat, load_hl)
    wait_all(copies[3:])
    off_ref[...] = offsets_of(donors_ref[...], table_ref[...])
    set_cell_cat(f_ref[...], off_ref[...], cell_cat)
    wait_all(blocks)


def start_loads(sources, places, sems):
    size = sources[0].shape[0] // 4
    copies = []
    for r in range(0, sources[0].shape[0], size):
        at = pl.ds(r, size)
        copies.append(pltpu.make_async_copy(sources[0].at[at], places[0].at[at], sems.at[len(copies)]))
    for source, place in zip(sources[1:], places[1:]):
        copies.append(pltpu.make_async_copy(source, place, sems.at[len(copies)]))
    return start_all(copies[::-1])


def load_kernel(after_ref, *refs):
    del after_ref
    *refs, sems = refs
    half = len(refs) // 2
    wait_all(start_loads(refs[:half], refs[half:], sems))


def load_for_genes_kernel(after_ref, *refs):
    del after_ref
    sources, places, (load_cat, l_ref, sems) = refs[:5], refs[5:9], refs[9:]
    copies = start_loads(sources, (*places, l_ref), sems)
    copies[0].wait()
    load_cat[...] = gene_operand(l_ref[...])
    wait_all(copies[1:])


def load_for_cells_kernel(after_ref, off_ref, *refs):
    del after_ref
    sources, places, (cell_cat, f_ref, sems) = refs[:5], refs[5:9], refs[9:]
    copies = start_loads(sources, (*places, f_ref), sems)
    copies[0].wait()
    set_cell_cat(f_ref[...], off_ref[...], cell_cat)
    wait_all(copies[1:])


class Stream:
    def __init__(self, copies, ahead=3):
        self.copies, self.ahead, self.done = copies, ahead, 0
        start_all(copies[:ahead])

    def need(self, count):
        while self.done < count:
            self.copies[self.done].wait()
            start_all(self.copies[self.done + self.ahead : self.done + self.ahead + 1])
            self.done += 1


def first_kernel(
    after_ref, tile_ref, load_cat, load_hl, cell_cat, front, counts_hbm, ga_ref, gb_ref, narrow_hbm,
    held, narrow, sems, out_sems, *, genes_total
):
    del after_ref
    begin = front.shape[0]
    copies = []
    for r in range(0, held.shape[0], COPY_CELLS):
        copies.append(
            pltpu.make_async_copy(
                counts_hbm.at[pl.ds(begin + r, COPY_CELLS)], held.at[pl.ds(r, COPY_CELLS)], sems.at[r // COPY_CELLS]
            )
        )
    stream = Stream(copies)
    ga_ref[ga_ref.shape[0] - SUB :, :] = tile_ref[...]
    kept = []

    def block(b):
        place = front if b == 0 else held.at[pl.ds(b * CELL_BLOCK - begin, CELL_BLOCK)]
        if len(kept) == b:
            stream.need(max(0, (b + 1) * CELL_BLOCK - begin) // COPY_CELLS)
            for g in range(0, place.shape[1], CHUNK):
                narrow[b, :, g : g + CHUNK] = place[:, g : g + CHUNK].astype(NARROW)
            kept.append(
                pltpu.make_async_copy(narrow.at[b], narrow_hbm.at[pl.ds(b * CELL_BLOCK, CELL_BLOCK)], out_sems.at[b])
            )
            kept[-1].start()
        return place

    cell_pass(cell_cat, load_cat, load_hl, block, (ga_ref, gb_ref), genes_total, FIRST_LOW_CHUNKS)
    wait_all(kept)


def out_copies(moved, outs, sems):
    return [pltpu.make_async_copy(moved.at[i], out, sems.at[i]) for i, out in enumerate(outs)]


def gene_kernel(
    tile_ref, ga_ref, gb_ref, off_ref, counts, f_ref, fm_ref, fv_ref, load_cat,
    la_ref, lb_ref, nf_hbm, nm_hbm, nv_hbm, moved, cell_cat, cell_hl, sems, *, cells_total
):
    held = f_ref, fm_ref, fv_ref
    width, cells = moved.shape[1:]
    half = cells // LANES // 2
    tile = move(
        held, lambda c: (ga_ref if c < half else gb_ref)[c % half * width : (c % half + 1) * width, :],
        jnp.sum(tile_ref[...]), cells_total * width, rate_factors, moved,
    )
    copies = start_all(out_copies(moved, (nf_hbm, nm_hbm, nv_hbm), sems))
    rows = la_ref.shape[1]
    for h in range(2):
        la_ref[h, rows - SUB : rows, :] = tile
    set_cells(moved[0], off_ref[...], cell_cat, cell_hl)
    gene_pass(load_cat, cell_cat, cell_hl, counts, (la_ref, lb_ref), cells_total)
    wait_all(copies)


def loading_rows(la_ref, lb_ref, width, genes):
    per = genes // LANES // 4

    def grad_row(c):
        q = c // per
        return (la_ref, lb_ref)[q // 2][q % 2, c % per * width : (c % per + 1) * width, :]

    return grad_row


def cell_kernel(
    tile_ref, la_ref, lb_ref, counts, l_ref, lm_ref, lv_ref, cell_cat,
    ga_ref, gb_ref, nl_hbm, nm_hbm, nv_hbm, moved, load_cat, load_hl, sems, *, genes_total
):
    held = l_ref, lm_ref, lv_ref
    width, genes = moved.shape[1:]
    tile = move(
        held, loading_rows(la_ref, lb_ref, width, genes), jnp.sum(tile_ref[...]), genes_total * width, rate_loadings, moved
    )
    copies = start_all(out_copies(moved, (nl_hbm, nm_hbm, nv_hbm), sems))
    ga_ref[ga_ref.shape[0] - SUB :, :] = tile
    set_loads(moved[0], load_cat, load_hl)
    block = lambda b: counts.at[pl.ds(b * CELL_BLOCK, CELL_BLOCK)]
    cell_pass(cell_cat, load_cat, load_hl, block, (ga_ref, gb_ref), genes_total, 0)
    wait_all(copies)


def last_kernel(
    tile_ref, la_ref, lb_ref, l_ref, lm_ref, lv_ref, nl_hbm, nm_hbm, nv_hbm, moved, sems, *, genes_total
):
    width, genes = moved.shape[1:]
    half = genes // 2
    total = jnp.sum(tile_ref[...])
    rows = loading_rows(la_ref, lb_ref, width, genes)
    copies = []
    for part in range(2):
        at = pl.ds(part * half, half)
        move(
            [ref.at[:, at] for ref in (l_ref, lm_ref, lv_ref)], lambda c: rows(c + part * half // LANES), total,
            genes_total * width, rate_loadings, moved.at[:, :, at],
        )
        for i, out in enumerate((nl_hbm, nm_hbm, nv_hbm)):
            copies.append(pltpu.make_async_copy(moved.at[i, :, at], out.at[:, at], sems.at[3 * part + i]))
        start_all(copies[-3:])
    wait_all(copies)


def exchange(value, partner):
    pairs = []
    for cell in range(32):
        for z in range(4):
            x, y, core, depth = partner(cell // 8, cell // 2 % 4, cell % 2, z)
            pairs.append((cell * 4 + z, ((x * 4 + y) * 2 + core) * 4 + depth))
    return lax.ppermute(value, ("cell", "gene"), pairs)


def near(i):
    return i ^ 1


def far(i):
    return 3 - i


def other_core(value):
    return exchange(value, lambda x, y, core, z: (x, y, 1 - core, z))


def along_cells(step):
    turn = near if step % 2 == 0 else far

    def partner(x, y, core, z):
        if (step // 2 + core) % 2 == 0:
            return turn(x), y, core, z
        return x, turn(y), core, z

    return partner


def along_genes(step):
    def partner(x, y, core, z):
        return x, y, core, (near if (step + core) % 2 == 0 else far)(z)

    return partner


def sum_over_chips(values, seen=None):
    for step in range(4):
        came = [exchange(v, along_cells(step ^ i)) for i, v in enumerate(values)]
        values = [v + c for v, c in zip(values, came)]
        if seen is not None:
            seen += values
    return values


def sum_over_cores(halves):
    core = lax.axis_index("cell") % 2
    keep = lax.dynamic_index_in_dim(halves, core, 0, keepdims=False)
    give = lax.dynamic_index_in_dim(halves, 1 - core, 0, keepdims=False)
    return keep + other_core(give)


def both_halves(own):
    core = lax.axis_index("cell") % 2
    theirs = other_core(own)
    return jnp.stack([jnp.where(core == 0, own, theirs), jnp.where(core == 0, theirs, own)])


def sum_over_cells(first, second):
    seen = []
    first, second = sum_over_chips([sum_over_cores(first), sum_over_cores(second)], seen)
    return both_halves(first), both_halves(second), seen


def on_device(counts, donors, offset_table, factors, factor_mean, factor_var, loadings, loading_mean, loading_var):
    width, cells = factors.shape
    genes = loadings.shape[1]
    cells_total = float(cells * lax.axis_size("cell"))
    genes_total = float(genes * lax.axis_size("gene"))
    vmem = pl.BlockSpec(memory_space=pltpu.VMEM)
    hbm = pl.BlockSpec(memory_space=pltpu.HBM)
    like = lambda *shape: jax.ShapeDtypeStruct(shape, f32)
    cell_rows = width * cells // LANES // 2
    gene_rows = width * genes // LANES // 4
    flops = 2 * (2 * DEPTH) * cells * genes
    dma = lambda n: pltpu.SemaphoreType.DMA((n,))
    in_vmem = lambda *shape: pltpu.VMEM(shape, f32)
    operand = lambda *shape: pltpu.VMEM(shape, bf16)
    three_f, three_l = [like(width, cells)] * 3, [like(width, genes)] * 3
    cell_grad = [like(cell_rows + SUB, LANES), like(cell_rows, LANES)]
    gene_grad = [like(2, gene_rows + SUB, LANES), like(2, gene_rows, LANES)]

    def call(kernel, name, ins, in_hbm, outs, out_hbm, scratch, work, moves=0, limit=12, **static):
        return pl.pallas_call(
            functools.partial(kernel, **static),
            name=name,
            in_specs=[vmem] * len(ins) + [hbm] * len(in_hbm),
            out_specs=[vmem] * len(outs) + [hbm] * len(out_hbm),
            out_shape=[pltpu.VMEM(o.shape, o.dtype) for o in outs] + [pltpu.HBM(o.shape, o.dtype) for o in out_hbm],
            scratch_shapes=list(scratch),
            compiler_params=pltpu.CompilerParams(vmem_limit_bytes=(limit << 20) if work else 6 << 20),
            cost_estimate=pl.CostEstimate(
                flops=int(flops * work), bytes_accessed=4 * width * cells + moves, transcendentals=int(cells * genes * work)
            ),
        )(
            *(pltpu.with_memory_space_constraint(x, pltpu.VMEM) for x in ins),
            *(pltpu.with_memory_space_constraint(x, pltpu.HBM) for x in in_hbm),
        )

    def shapes(arrays):
        return [jax.ShapeDtypeStruct(a.shape, a.dtype) for a in arrays]

    def bring_for_genes(after, *arrays):
        return call(
            load_for_genes_kernel, "load_for_genes", [after], list(arrays),
            shapes(arrays[:4]) + [jax.ShapeDtypeStruct((DEPTH, genes), bf16)], [],
            [in_vmem(width, genes), dma(8)], 0, cells * genes + 16 * width * cells,
        )

    def bring_for_cells(after, off, *arrays):
        return call(
            load_for_cells_kernel, "load_for_cells", [after, off], list(arrays),
            shapes(arrays[:4]) + [jax.ShapeDtypeStruct((cells, DEPTH), bf16)], [],
            [in_vmem(width, cells), dma(8)], 0, cells * genes + 16 * width * cells,
        )

    def bring(after, *arrays):
        return call(
            load_kernel, "load", [after], list(arrays), shapes(arrays), [], [dma(len(arrays) + 3)], 0, 12 * width * cells
        )

    donor_row, table_row = donors.reshape(1, cells), offset_table.reshape(1, -1)
    operands = [jax.ShapeDtypeStruct((DEPTH, genes), bf16), jax.ShapeDtypeStruct((2 * width, genes), bf16)]
    fac_tile, load_tile, off, *ready = call(
        front_kernel, "front", [],
        [factor_var, loading_var, loadings, donor_row, table_row, factors, counts],
        [like(SUB, LANES), like(SUB, LANES), like(1, cells), *operands, jax.ShapeDtypeStruct((cells, DEPTH), bf16), like(CELL_BLOCK, genes)], [],
        [
            in_vmem(width, cells), in_vmem(width, genes), in_vmem(width, genes),
            pltpu.VMEM((1, cells), jnp.int32), pltpu.VMEM((1, table_row.shape[1]), jnp.int32),
            in_vmem(width, cells), dma(10),
        ],
        0, 4 * CELL_BLOCK * genes,
    )
    fac_tile = fac_tile + other_core(fac_tile)
    blocks = cells // CELL_BLOCK
    rest = cells - CELL_BLOCK
    grad_a, grad_b, narrow = call(
        first_kernel, "cell_pass_first", [fac_tile, load_tile, *ready], [counts],
        cell_grad, [jax.ShapeDtypeStruct((cells, genes), NARROW)],
        [
            in_vmem(rest, genes), pltpu.VMEM((blocks, CELL_BLOCK, genes), NARROW), dma(rest // COPY_CELLS), dma(blocks),
        ],
        1.5, limit=32, genes_total=genes_total,
    )

    def loading_gradient(fac_tile, grad_a, grad_b, held):
        first, second, *new = call(
            gene_kernel, "gene_pass", [fac_tile, grad_a, grad_b, off, *held], [], gene_grad, three_f,
            [in_vmem(3, width, cells), operand(cells, DEPTH), operand(2 * width, cells), dma(3)], 1, cells_total=cells_total,
        )
        return first, second, new

    def factor_gradient(load_tile, grad_l, grad_m, held):
        first, second, *new = call(
            cell_kernel, "cell_pass", [load_tile, grad_l, grad_m, *held], [], cell_grad, three_l,
            [in_vmem(3, width, genes), operand(DEPTH, genes), operand(2 * width, genes), dma(3)], 1, genes_total=genes_total,
        )
        return first, second, new

    fac_tile = fac_tile + exchange(fac_tile, along_cells(0))
    grad_a, fac_tile = lax.optimization_barrier((grad_a, fac_tile))
    came_a, came_b = exchange(grad_a, along_genes(0)), exchange(grad_b, along_genes(0))
    for step in (1, 2):
        fac_tile = fac_tile + exchange(fac_tile, along_cells(step))
    fac_tile, grad_a, grad_b = lax.optimization_barrier((fac_tile, grad_a + came_a, grad_b + came_b))
    came_a, came_b = exchange(grad_a, along_genes(1)), exchange(grad_b, along_genes(1))
    held = bring_for_genes(grad_a, narrow, factors, factor_mean, factor_var, loadings)
    fac_tile = fac_tile + exchange(fac_tile, along_cells(3))
    grad_a, grad_b = grad_a + came_a, grad_b + came_b
    load_tile = grad_a[cell_rows:]
    grad_l, grad_m, f = loading_gradient(fac_tile, grad_a, grad_b, held)
    grad_l, grad_m, seen = sum_over_cells(grad_l, grad_m)
    fac_tile = grad_l[0, gene_rows:]
    held = bring_for_cells(seen[4], off, narrow, loadings, loading_mean, loading_var, f[0])
    grad_a, grad_b, l = factor_gradient(load_tile, grad_l, grad_m, held)
    came_a, came_b = exchange(grad_a, along_genes(0)), exchange(grad_b, along_genes(0))
    grad_a, grad_b = grad_a + came_a, grad_b + came_b
    came_a, came_b = exchange(grad_a, along_genes(1)), exchange(grad_b, along_genes(1))
    held = bring_for_genes(grad_a, narrow, *f, l[0])
    grad_a, grad_b = grad_a + came_a, grad_b + came_b
    load_tile = grad_a[cell_rows:]
    grad_l, grad_m, f = loading_gradient(fac_tile, grad_a, grad_b, held)
    grad_l, grad_m, seen = sum_over_cells(grad_l, grad_m)
    held = bring(seen[0], *l)
    l = call(
        last_kernel, "loading_move", [load_tile, grad_l, grad_m, *held], [], [], three_l, [in_vmem(3, width, genes), dma(6)],
        0, genes_total=genes_total,
    )
    return (*f, *l)


def solution(mesh):
    by_cell, by_gene = P(None, "cell"), P(None, "gene")
    return jax.shard_map(
        on_device,
        mesh=mesh,
        in_specs=(P("cell", "gene"), P("cell"), P(), by_cell, by_cell, by_cell, by_gene, by_gene, by_gene),
        out_specs=(by_cell, by_cell, by_cell, by_gene, by_gene, by_gene),
        check_vma=False,
    )
```

```python
import functools
import math

import jax
import jax.numpy as jnp
from jax import lax
from jax.experimental import pallas as pl
from jax.experimental.pallas import tpu as pltpu
from jax.sharding import PartitionSpec as P

decay_first = 0.9
decay_second = 0.999
epsilon = 1e-06
rate_factors = 0.2
rate_loadings = 0.2
offset_unit = 0.125
LOG2E = math.log2(math.e)
LANES = 128
SUB = 8
DEPTH = 256
f32 = jnp.float32
bf16 = jnp.bfloat16
CELL_BLOCK = 512
GENE_BLOCK = 512
COPY_CELLS = 256
PARTS = 2
CHUNK = 512
FIRST_LOW_CHUNKS = 2
NARROW = jnp.float8_e4m3fn


def split(x):
    high = x.astype(bf16)
    return high, (x - high.astype(f32)).astype(bf16)


def inverse_root(variance):
    return 1.0 / (jnp.sqrt(variance) + epsilon)


def square_tile(scale):
    square = scale * scale
    total = None
    for r in range(0, scale.shape[0], SUB):
        for c in range(0, scale.shape[1], LANES):
            part = square[r : r + SUB, c : c + LANES]
            total = part if total is None else total + part
    return total


def cell_operand(f, off):
    high, low = split(f)
    first = off.astype(bf16).astype(f32)
    rest = off - first
    second = rest.astype(bf16).astype(f32)
    third = rest - second
    row = lax.broadcasted_iota(jnp.int32, f.shape, 0)
    extra = jnp.where(row == 0, first, jnp.where(row == 1, second, jnp.where(row == 2, third, 0.0)))
    return high, low, jnp.concatenate([high, high, low, extra.astype(bf16)], 0)


def gene_operand(l):
    high, low = split(l * LOG2E)
    row = lax.broadcasted_iota(jnp.int32, l.shape, 0)
    ones = jnp.where(row < 3, 1.0, 0.0).astype(bf16)
    return jnp.concatenate([high, low, high, ones], 0)


def offsets_of(donors, table):
    column = jnp.broadcast_to(table.astype(f32), (LANES, table.shape[1])).T[:, :1]
    which = lax.broadcasted_iota(jnp.int32, (table.shape[1], donors.shape[1]), 0)
    picked = jnp.where(which == donors, column, 0.0)
    return jnp.sum(picked, axis=0, keepdims=True) * (offset_unit * LOG2E)


def set_loads(l, load_cat, load_hl):
    load_cat[...] = gene_operand(l)
    high, low = split(l)
    load_hl[...] = jnp.concatenate([high, low], 0)


def set_cell_cat(f, off, cell_cat):
    _, _, cat = cell_operand(f, off)
    cell_cat[...] = cat.T


def set_cells(f, off, cell_cat, cell_hl):
    high, low, cat = cell_operand(f, off)
    cell_cat[...] = cat.T
    cell_hl[...] = jnp.concatenate([high, low], 0)


def lane_rows(grad):
    return jnp.concatenate([grad[:, c : c + LANES] for c in range(0, grad.shape[1], LANES)], 0)


def wait_all(copies):
    for copy in copies:
        copy.wait()


def start_all(copies):
    for copy in copies:
        copy.start()
    return copies


def cell_pass(cell_cat, load_cat, load_hl, counts, g_refs, genes_total, low_chunks):
    cells, genes = cell_cat.shape[0], load_cat.shape[1]
    width = load_hl.shape[0] // 2
    blocks = cells // CELL_BLOCK
    rows = width * CELL_BLOCK // LANES
    last = (((1,), (1,)), ((), ()))
    for b in range(blocks):
        lhs = cell_cat[b * CELL_BLOCK : (b + 1) * CELL_BLOCK, :]
        held = counts(b)

        def lin_of(g):
            return jnp.dot(lhs, load_cat[:, g : g + CHUNK], preferred_element_type=f32)

        total, small = None, None
        lin = lin_of(0)
        for g in range(0, genes, CHUNK):
            of = slice(g, g + CHUNK)
            resid = jnp.exp2(lin) - held[:, of].astype(f32)
            if low_chunks and g + CHUNK < genes:
                lin = lin_of(g + CHUNK)
            high, low = split(resid)
            part = lax.dot_general(load_hl[:, of], high, last, preferred_element_type=f32)
            total = part if total is None else total + part
            if g // CHUNK < low_chunks:
                part = lax.dot_general(load_hl[:width, of], low, last, preferred_element_type=f32)
                small = part if small is None else small + part
            if not low_chunks and g + CHUNK < genes:
                lin = lin_of(g + CHUNK)
        grad = total[:width] + total[width:]
        if low_chunks:
            grad += small
        half = blocks // 2
        g_refs[b // half][b % half * rows : (b % half + 1) * rows, :] = lane_rows(grad * (1.0 / math.sqrt(genes_total)))


def gene_pass(load_cat, cell_cat, cell_hl, counts, g_refs, cells_total):
    width, genes = cell_hl.shape[0] // 2, load_cat.shape[1]
    blocks = genes // GENE_BLOCK
    rows = width * GENE_BLOCK // LANES
    quarter = blocks // 4
    for b in range(blocks):
        at = slice(b * GENE_BLOCK, (b + 1) * GENE_BLOCK)
        load = load_cat[:, at]
        total = None
        lin = jnp.dot(cell_cat[:CHUNK, :], load, preferred_element_type=f32)
        for c in range(0, cell_cat.shape[0], CHUNK):
            of = slice(c, c + CHUNK)
            resid = (jnp.exp2(lin) - counts[of, at].astype(f32)).astype(bf16)
            if c + CHUNK < cell_cat.shape[0]:
                lin = jnp.dot(cell_cat[c + CHUNK : c + 2 * CHUNK, :], load, preferred_element_type=f32)
            part = jnp.dot(cell_hl[:, of], resid, preferred_element_type=f32)
            total = part if total is None else total + part
        grad = (total[:width] + total[width:]) * (1.0 / math.sqrt(cells_total))
        q = b // quarter
        g_refs[q // 2][q % 2, b % quarter * rows : (b % quarter + 1) * rows, :] = lane_rows(grad)


def move(held, grad_row, total, entries, rate, moved):
    factor = rate / jnp.sqrt(total / entries)
    tile = None
    for c in range(0, moved.shape[2], LANES):
        at = slice(c, c + LANES)
        gradient = grad_row(c // LANES)
        var_old = held[2][:, at]
        mean = decay_first * held[1][:, at] + (1.0 - decay_first) * gradient
        var = decay_second * var_old + (1.0 - decay_second) * gradient * gradient
        moved[0, :, at] = held[0][:, at] - factor * mean * inverse_root(var_old)
        moved[1, :, at] = mean
        moved[2, :, at] = var
        part = square_tile(inverse_root(var))
        tile = part if tile is None else tile + part
    return tile


def front_kernel(
    fv_hbm, lv_hbm, l_hbm, donors_hbm, table_hbm, f_hbm, counts_hbm,
    fac_ref, load_ref, off_ref, load_cat, load_hl, cell_cat, front, fv_ref, lv_ref, l_ref, donors_ref, table_ref, f_ref, sems
):
    pairs = [
        (fv_hbm, fv_ref), (lv_hbm, lv_ref), (l_hbm, l_ref), (donors_hbm, donors_ref), (table_hbm, table_ref), (f_hbm, f_ref)
    ]
    copies = start_all([pltpu.make_async_copy(src, dst, sems.at[i]) for i, (src, dst) in enumerate(pairs)])
    size = front.shape[0] // 4
    blocks = []
    for b in range(4):
        at = pl.ds(b * size, size)
        blocks.append(pltpu.make_async_copy(counts_hbm.at[at], front.at[at], sems.at[len(pairs) + b]))
    start_all(blocks)
    copies[0].wait()
    fac_ref[...] = square_tile(inverse_root(fv_ref[...]))
    copies[1].wait()
    load_ref[...] = square_tile(inverse_root(lv_ref[...]))
    copies[2].wait()
    set_loads(l_ref[...], load_cat, load_hl)
    wait_all(copies[3:])
    off_ref[...] = offsets_of(donors_ref[...], table_ref[...])
    set_cell_cat(f_ref[...], off_ref[...], cell_cat)
    wait_all(blocks)


def start_loads(sources, places, sems):
    size = sources[0].shape[0] // 4
    copies = []
    for r in range(0, sources[0].shape[0], size):
        at = pl.ds(r, size)
        copies.append(pltpu.make_async_copy(sources[0].at[at], places[0].at[at], sems.at[len(copies)]))
    for source, place in zip(sources[1:], places[1:]):
        copies.append(pltpu.make_async_copy(source, place, sems.at[len(copies)]))
    return start_all(copies[::-1])


def load_kernel(after_ref, *refs):
    del after_ref
    *refs, sems = refs
    half = len(refs) // 2
    wait_all(start_loads(refs[:half], refs[half:], sems))


def load_for_genes_kernel(after_ref, *refs):
    del after_ref
    sources, places, (load_cat, l_ref, sems) = refs[:5], refs[5:9], refs[9:]
    copies = start_loads(sources, (*places, l_ref), sems)
    copies[0].wait()
    load_cat[...] = gene_operand(l_ref[...])
    wait_all(copies[1:])


def load_for_cells_kernel(after_ref, off_ref, *refs):
    del after_ref
    sources, places, (cell_cat, f_ref, sems) = refs[:5], refs[5:9], refs[9:]
    copies = start_loads(sources, (*places, f_ref), sems)
    copies[0].wait()
    set_cell_cat(f_ref[...], off_ref[...], cell_cat)
    wait_all(copies[1:])


class Stream:
    def __init__(self, copies, ahead=3):
        self.copies, self.ahead, self.done = copies, ahead, 0
        start_all(copies[:ahead])

    def need(self, count):
        while self.done < count:
            self.copies[self.done].wait()
            start_all(self.copies[self.done + self.ahead : self.done + self.ahead + 1])
            self.done += 1


def first_kernel(
    after_ref, tile_ref, load_cat, load_hl, cell_cat, front, counts_hbm, ga_ref, gb_ref, narrow_hbm,
    held, narrow, sems, out_sems, *, genes_total
):
    del after_ref
    begin = front.shape[0]
    copies = []
    for r in range(0, held.shape[0], COPY_CELLS):
        copies.append(
            pltpu.make_async_copy(
                counts_hbm.at[pl.ds(begin + r, COPY_CELLS)], held.at[pl.ds(r, COPY_CELLS)], sems.at[r // COPY_CELLS]
            )
        )
    stream = Stream(copies)
    ga_ref[ga_ref.shape[0] - SUB :, :] = tile_ref[...]
    kept = []

    def block(b):
        place = front if b == 0 else held.at[pl.ds(b * CELL_BLOCK - begin, CELL_BLOCK)]
        if len(kept) == b:
            stream.need(max(0, (b + 1) * CELL_BLOCK - begin) // COPY_CELLS)
            for g in range(0, place.shape[1], CHUNK):
                narrow[b, :, g : g + CHUNK] = place[:, g : g + CHUNK].astype(NARROW)
            kept.append(
                pltpu.make_async_copy(narrow.at[b], narrow_hbm.at[pl.ds(b * CELL_BLOCK, CELL_BLOCK)], out_sems.at[b])
            )
            kept[-1].start()
        return place

    cell_pass(cell_cat, load_cat, load_hl, block, (ga_ref, gb_ref), genes_total, FIRST_LOW_CHUNKS)
    wait_all(kept)


def out_copies(moved, outs, sems):
    return [pltpu.make_async_copy(moved.at[i], out, sems.at[i]) for i, out in enumerate(outs)]


def gene_kernel(
    tile_ref, ga_ref, gb_ref, off_ref, counts, f_ref, fm_ref, fv_ref, load_cat,
    la_ref, lb_ref, nf_hbm, nm_hbm, nv_hbm, moved, cell_cat, cell_hl, sems, *, cells_total
):
    held = f_ref, fm_ref, fv_ref
    width, cells = moved.shape[1:]
    half = cells // LANES // 2
    tile = move(
        held, lambda c: (ga_ref if c < half else gb_ref)[c % half * width : (c % half + 1) * width, :],
        jnp.sum(tile_ref[...]), cells_total * width, rate_factors, moved,
    )
    copies = start_all(out_copies(moved, (nf_hbm, nm_hbm, nv_hbm), sems))
    rows = la_ref.shape[1]
    for h in range(2):
        la_ref[h, rows - SUB : rows, :] = tile
    set_cells(moved[0], off_ref[...], cell_cat, cell_hl)
    gene_pass(load_cat, cell_cat, cell_hl, counts, (la_ref, lb_ref), cells_total)
    wait_all(copies)


def loading_rows(la_ref, lb_ref, width, genes):
    per = genes // LANES // 4

    def grad_row(c):
        q = c // per
        return (la_ref, lb_ref)[q // 2][q % 2, c % per * width : (c % per + 1) * width, :]

    return grad_row


def cell_kernel(
    tile_ref, la_ref, lb_ref, counts, l_ref, lm_ref, lv_ref, cell_cat,
    ga_ref, gb_ref, nl_hbm, nm_hbm, nv_hbm, moved, load_cat, load_hl, sems, *, genes_total
):
    held = l_ref, lm_ref, lv_ref
    width, genes = moved.shape[1:]
    tile = move(
        held, loading_rows(la_ref, lb_ref, width, genes), jnp.sum(tile_ref[...]), genes_total * width, rate_loadings, moved
    )
    copies = start_all(out_copies(moved, (nl_hbm, nm_hbm, nv_hbm), sems))
    ga_ref[ga_ref.shape[0] - SUB :, :] = tile
    set_loads(moved[0], load_cat, load_hl)
    block = lambda b: counts.at[pl.ds(b * CELL_BLOCK, CELL_BLOCK)]
    cell_pass(cell_cat, load_cat, load_hl, block, (ga_ref, gb_ref), genes_total, 0)
    wait_all(copies)


def last_kernel(
    tile_ref, la_ref, lb_ref, l_ref, lm_ref, lv_ref, nl_hbm, nm_hbm, nv_hbm, moved, sems, *, genes_total
):
    width, genes = moved.shape[1:]
    half = genes // 2
    total = jnp.sum(tile_ref[...])
    rows = loading_rows(la_ref, lb_ref, width, genes)
    copies = []
    for part in range(2):
        at = pl.ds(part * half, half)
        move(
            [ref.at[:, at] for ref in (l_ref, lm_ref, lv_ref)], lambda c: rows(c + part * half // LANES), total,
            genes_total * width, rate_loadings, moved.at[:, :, at],
        )
        for i, out in enumerate((nl_hbm, nm_hbm, nv_hbm)):
            copies.append(pltpu.make_async_copy(moved.at[i, :, at], out.at[:, at], sems.at[3 * part + i]))
        start_all(copies[-3:])
    wait_all(copies)


def exchange(value, partner):
    pairs = []
    for cell in range(32):
        for z in range(4):
            x, y, core, depth = partner(cell // 8, cell // 2 % 4, cell % 2, z)
            pairs.append((cell * 4 + z, ((x * 4 + y) * 2 + core) * 4 + depth))
    return lax.ppermute(value, ("cell", "gene"), pairs)


def near(i):
    return i ^ 1


def far(i):
    return 3 - i


def other_core(value):
    return exchange(value, lambda x, y, core, z: (x, y, 1 - core, z))


def along_cells(step):
    turn = near if step % 2 == 0 else far

    def partner(x, y, core, z):
        if (step // 2 + core) % 2 == 0:
            return turn(x), y, core, z
        return x, turn(y), core, z

    return partner


def along_genes(step):
    def partner(x, y, core, z):
        return x, y, core, (near if (step + core) % 2 == 0 else far)(z)

    return partner


def sum_over_chips(values, seen=None):
    for step in range(4):
        came = [exchange(v, along_cells(step ^ i)) for i, v in enumerate(values)]
        values = [v + c for v, c in zip(values, came)]
        if seen is not None:
            seen += values
    return values


def sum_over_cores(halves):
    core = lax.axis_index("cell") % 2
    keep = lax.dynamic_index_in_dim(halves, core, 0, keepdims=False)
    give = lax.dynamic_index_in_dim(halves, 1 - core, 0, keepdims=False)
    return keep + other_core(give)


def both_halves(own):
    core = lax.axis_index("cell") % 2
    theirs = other_core(own)
    return jnp.stack([jnp.where(core == 0, own, theirs), jnp.where(core == 0, theirs, own)])


def sum_over_cells(first, second):
    seen = []
    first, second = sum_over_chips([sum_over_cores(first), sum_over_cores(second)], seen)
    return both_halves(first), both_halves(second), seen


def on_device(counts, donors, offset_table, factors, factor_mean, factor_var, loadings, loading_mean, loading_var):
    width, cells = factors.shape
    genes = loadings.shape[1]
    cells_total = float(cells * lax.axis_size("cell"))
    genes_total = float(genes * lax.axis_size("gene"))
    vmem = pl.BlockSpec(memory_space=pltpu.VMEM)
    hbm = pl.BlockSpec(memory_space=pltpu.HBM)
    like = lambda *shape: jax.ShapeDtypeStruct(shape, f32)
    cell_rows = width * cells // LANES // 2
    gene_rows = width * genes // LANES // 4
    flops = 2 * (2 * DEPTH) * cells * genes
    dma = lambda n: pltpu.SemaphoreType.DMA((n,))
    in_vmem = lambda *shape: pltpu.VMEM(shape, f32)
    operand = lambda *shape: pltpu.VMEM(shape, bf16)
    three_f, three_l = [like(width, cells)] * 3, [like(width, genes)] * 3
    cell_grad = [like(cell_rows + SUB, LANES), like(cell_rows, LANES)]
    gene_grad = [like(2, gene_rows + SUB, LANES), like(2, gene_rows, LANES)]

    def call(kernel, name, ins, in_hbm, outs, out_hbm, scratch, work, moves=0, limit=12, **static):
        return pl.pallas_call(
            functools.partial(kernel, **static),
            name=name,
            in_specs=[vmem] * len(ins) + [hbm] * len(in_hbm),
            out_specs=[vmem] * len(outs) + [hbm] * len(out_hbm),
            out_shape=[pltpu.VMEM(o.shape, o.dtype) for o in outs] + [pltpu.HBM(o.shape, o.dtype) for o in out_hbm],
            scratch_shapes=list(scratch),
            compiler_params=pltpu.CompilerParams(vmem_limit_bytes=(limit << 20) if work else 6 << 20),
            cost_estimate=pl.CostEstimate(
                flops=int(flops * work), bytes_accessed=4 * width * cells + moves, transcendentals=int(cells * genes * work)
            ),
        )(
            *(pltpu.with_memory_space_constraint(x, pltpu.VMEM) for x in ins),
            *(pltpu.with_memory_space_constraint(x, pltpu.HBM) for x in in_hbm),
        )

    def shapes(arrays):
        return [jax.ShapeDtypeStruct(a.shape, a.dtype) for a in arrays]

    def bring_for_genes(after, *arrays):
        return call(
            load_for_genes_kernel, "load_for_genes", [after], list(arrays),
            shapes(arrays[:4]) + [jax.ShapeDtypeStruct((DEPTH, genes), bf16)], [],
            [in_vmem(width, genes), dma(8)], 0, cells * genes + 16 * width * cells,
        )

    def bring_for_cells(after, off, *arrays):
        return call(
            load_for_cells_kernel, "load_for_cells", [after, off], list(arrays),
            shapes(arrays[:4]) + [jax.ShapeDtypeStruct((cells, DEPTH), bf16)], [],
            [in_vmem(width, cells), dma(8)], 0, cells * genes + 16 * width * cells,
        )

    def bring(after, *arrays):
        return call(
            load_kernel, "load", [after], list(arrays), shapes(arrays), [], [dma(len(arrays) + 3)], 0, 12 * width * cells
        )

    donor_row, table_row = donors.reshape(1, cells), offset_table.reshape(1, -1)
    operands = [jax.ShapeDtypeStruct((DEPTH, genes), bf16), jax.ShapeDtypeStruct((2 * width, genes), bf16)]
    fac_tile, load_tile, off, *ready = call(
        front_kernel, "front", [],
        [factor_var, loading_var, loadings, donor_row, table_row, factors, counts],
        [like(SUB, LANES), like(SUB, LANES), like(1, cells), *operands, jax.ShapeDtypeStruct((cells, DEPTH), bf16), like(CELL_BLOCK, genes)], [],
        [
            in_vmem(width, cells), in_vmem(width, genes), in_vmem(width, genes),
            pltpu.VMEM((1, cells), jnp.int32), pltpu.VMEM((1, table_row.shape[1]), jnp.int32),
            in_vmem(width, cells), dma(10),
        ],
        0, 4 * CELL_BLOCK * genes,
    )
    fac_tile = fac_tile + other_core(fac_tile)
    blocks = cells // CELL_BLOCK
    rest = cells - CELL_BLOCK
    grad_a, grad_b, narrow = call(
        first_kernel, "cell_pass_first", [fac_tile, load_tile, *ready], [counts],
        cell_grad, [jax.ShapeDtypeStruct((cells, genes), NARROW)],
        [
            in_vmem(rest, genes), pltpu.VMEM((blocks, CELL_BLOCK, genes), NARROW), dma(rest // COPY_CELLS), dma(blocks),
        ],
        1.5, limit=32, genes_total=genes_total,
    )

    def loading_gradient(fac_tile, grad_a, grad_b, held):
        first, second, *new = call(
            gene_kernel, "gene_pass", [fac_tile, grad_a, grad_b, off, *held], [], gene_grad, three_f,
            [in_vmem(3, width, cells), operand(cells, DEPTH), operand(2 * width, cells), dma(3)], 1, cells_total=cells_total,
        )
        return first, second, new

    def factor_gradient(load_tile, grad_l, grad_m, held):
        first, second, *new = call(
            cell_kernel, "cell_pass", [load_tile, grad_l, grad_m, *held], [], cell_grad, three_l,
            [in_vmem(3, width, genes), operand(DEPTH, genes), operand(2 * width, genes), dma(3)], 1, genes_total=genes_total,
        )
        return first, second, new

    fac_tile = fac_tile + exchange(fac_tile, along_cells(0))
    grad_a, fac_tile = lax.optimization_barrier((grad_a, fac_tile))
    came_a, came_b = exchange(grad_a, along_genes(0)), exchange(grad_b, along_genes(0))
    for step in (1, 2):
        fac_tile = fac_tile + exchange(fac_tile, along_cells(step))
    fac_tile, grad_a, grad_b = lax.optimization_barrier((fac_tile, grad_a + came_a, grad_b + came_b))
    came_a, came_b = exchange(grad_a, along_genes(1)), exchange(grad_b, along_genes(1))
    held = bring_for_genes(grad_a, narrow, factors, factor_mean, factor_var, loadings)
    fac_tile = fac_tile + exchange(fac_tile, along_cells(3))
    grad_a, grad_b = grad_a + came_a, grad_b + came_b
    load_tile = grad_a[cell_rows:]
    grad_l, grad_m, f = loading_gradient(fac_tile, grad_a, grad_b, held)
    grad_l, grad_m, seen = sum_over_cells(grad_l, grad_m)
    fac_tile = grad_l[0, gene_rows:]
    held = bring_for_cells(seen[4], off, narrow, loadings, loading_mean, loading_var, f[0])
    grad_a, grad_b, l = factor_gradient(load_tile, grad_l, grad_m, held)
    came_a, came_b = exchange(grad_a, along_genes(0)), exchange(grad_b, along_genes(0))
    grad_a, grad_b = grad_a + came_a, grad_b + came_b
    came_a, came_b = exchange(grad_a, along_genes(1)), exchange(grad_b, along_genes(1))
    held = bring_for_genes(grad_a, narrow, *f, l[0])
    grad_a, grad_b = grad_a + came_a, grad_b + came_b
    load_tile = grad_a[cell_rows:]
    grad_l, grad_m, f = loading_gradient(fac_tile, grad_a, grad_b, held)
    grad_l, grad_m, seen = sum_over_cells(grad_l, grad_m)
    held = bring(seen[0], *l)
    l = call(
        last_kernel, "loading_move", [load_tile, grad_l, grad_m, *held], [], [], three_l, [in_vmem(3, width, genes), dma(6)],
        0, genes_total=genes_total,
    )
    return (*f, *l)


def solution(mesh):
    by_cell, by_gene = P(None, "cell"), P(None, "gene")
    return jax.shard_map(
        on_device,
        mesh=mesh,
        in_specs=(P("cell", "gene"), P("cell"), P(), by_cell, by_cell, by_cell, by_gene, by_gene, by_gene),
        out_specs=(by_cell, by_cell, by_cell, by_gene, by_gene, by_gene),
        check_vma=False,
    )
```
